256 devices in a mesh: gz: 128 (over y, x_lo, z, core), gy: 2 (over x_hi).
Axes of the slice: x: 4 (x_hi: 2, x_lo: 2; x = x_hi * 2 + x_lo), y: 4, z: 8, core: 2. Of those that a mesh axis runs over, the one named last changes fastest.
Arguments:
- sensitivity: float32 [1024, 128, 512], P('gz', 'gy'), may hold values from -70 to 70
- density: float32 [1024, 128, 512], P('gz', 'gy'), may hold values from 0 to 1
- load: float32 [1024, 128, 512], P('gz', 'gy'), may hold values from -6 to 6
- adjoint: float32 [1024, 128, 512], P('gz', 'gy'), may hold values from -6 to 6
- labels: int32 [1024, 128, 512], P('gz', 'gy'), may hold values from 0 to 2
Outputs:
- update_direction: float32 [1024, 128, 512], P('gz', 'gy')
- adjoint_next: float32 [1024, 128, 512], P('gz', 'gy')
The draws below stay inside these ranges and needn't reach their ends.
Inputs may be any that keep to these rules, and one draw needn't show every extreme that they name: `labels`: 0 marks a design voxel, 1 fixed masonry, 2 a supported voxel.
All inputs are finite; a program needn't handle non-finite values.
Results may differ from the reference program's by a relative error of at most 0.0003.
Values sent between devices are 32-bit elements; how exact they have to be, the bound alone decides.
A program may use at most 64 MiB of HBM per device.

```python
import math
import jax
import jax.numpy as jnp

CZ = 8
CY = 64
NX = 512
ITERS = 4
NZ = 1024
NY = 128


def height_ramp():
    height = jnp.arange(NZ, dtype=jnp.float32) / max(NZ - 1, 1)
    return ((1.0 + 2.0 * height) / 3.0)[:, None, None]


def block_loudness(key, low, high):
    blocks = jax.random.uniform(key, (NZ // CZ, NY // CY), jnp.float32, low, high)
    factor = jnp.exp(blocks)
    factor = jnp.repeat(jnp.repeat(factor, CZ, axis=0), CY, axis=1)
    return factor[:, :, None]


def draw_density(key, part):
    key = jax.random.fold_in(key, 1)
    first, second = jax.random.split(key)
    ramp = height_ramp()
    loudness = block_loudness(second, -0.7, 0.0)
    base = jax.random.uniform(first, (NZ, NY, NX), jnp.float32, 0.3, 1.0)
    return (base * ramp * loudness).astype(jnp.float32)


def draw_sensitivity(key, part):
    key = jax.random.fold_in(key, 2)
    first, second = jax.random.split(key)
    third = jax.random.fold_in(key, 7)
    ramp = height_ramp()
    columns = jnp.exp(math.log(10.0) * jax.random.uniform(second, (1, NY, NX), jnp.float32))
    loudness = block_loudness(third, -0.7, 0.7)
    base = jnp.clip(jax.random.normal(first, (NZ, NY, NX), jnp.float32), -5.0, 5.0)
    values = base * columns * ramp * loudness
    return jnp.clip(values, -70.0, 70.0).astype(jnp.float32)


def plant(values, stream_key, low, top_value):
    index_at = [jax.random.randint(jax.random.fold_in(stream_key, axis), (), 0, length) for axis, length in enumerate(values.shape)]
    main_axis = values.shape.index(max(values.shape))
    neighbour = index_at[:main_axis] + [(index_at[main_axis] + 1) % values.shape[main_axis]] + index_at[main_axis + 1:]
    return values.at[tuple(index_at)].set(low).at[tuple(neighbour)].set(top_value)


def steps_of(rng, extent, shards, smallest, top_value):
    level, own = 1.0, jax.random.fold_in(rng, 6)
    for dim, blocks in shards:
        heights = jnp.exp(jax.random.uniform(jax.random.fold_in(own, dim), (blocks,), jnp.float32, smallest / len(shards), top_value / len(shards)))
        level = level * jnp.repeat(heights, extent[dim] // blocks).reshape([-1 if axis == dim else 1 for axis in range(len(extent))])
    return level


def noise(stream_key, dims, scale, reach, pieces=(), held_as=jnp.bfloat16):
    array = jax.random.normal(stream_key, dims, jnp.float32) * scale
    if len(pieces) > 0:
        array = steps_of(stream_key, dims, pieces, -0.22, 0.18) * array
    return jnp.clip(array, min=-reach, max=reach).astype(held_as)


def setup_inputs(seed: int = 0) -> dict:
    key_list = jax.random.split(jax.random.key(seed), 6)
    sensitivity = draw_sensitivity(jax.random.fold_in(key_list[5], 71), 0)
    density = draw_density(jax.random.fold_in(key_list[5], 71), 0)
    load = noise(key_list[2], (NZ, NY, NX), 1.0, 6.0, ((0, 128), (1, 2)), jnp.float32)
    adjoint = noise(key_list[3], (NZ, NY, NX), 1.0, 6.0, ((0, 128), (1, 2)), jnp.float32)
    labels = plant(jax.random.randint(key_list[4], (NZ, NY, NX), 0, 3), jax.random.fold_in(key_list[4], 1), 0, 2).astype(jnp.int32)
    return {"sensitivity": sensitivity, "density": density, "load": load, "adjoint": adjoint, "labels": labels}


filter_weight = 8.0
stiff_floor = 0.05
relax_omega = 0.6
volume_target = 0.15
volume_penalty = 20.0
epsilon = 1e-6
center_diag = 1.0 + 6.0 * filter_weight
lower_eig = 1.0 / center_diag
upper_eig = (1.0 + 12.0 * filter_weight) / center_diag
middle_eig = (upper_eig + lower_eig) / 2.0
half_width = (upper_eig - lower_eig) / 2.0
sigma_ratio = middle_eig / half_width


def neighbour_sum(padded):
    total = padded[2:, 1:-1, 1:-1] + padded[:-2, 1:-1, 1:-1]
    total = total + padded[1:-1, 2:, 1:-1] + padded[1:-1, :-2, 1:-1]
    return total + padded[1:-1, 1:-1, 2:] + padded[1:-1, 1:-1, :-2]


def filter_apply(field):
    return center_diag * field - filter_weight * neighbour_sum(jnp.pad(field, 1))


def chebyshev(source):
    residue = source
    update = source / (center_diag * middle_eig)
    result = update
    ratio_prev = 1.0 / sigma_ratio
    for iteration in range(ITERS):
        residue = residue - filter_apply(update)
        ratio_next = 1.0 / (2.0 * sigma_ratio - ratio_prev)
        update = (ratio_next * ratio_prev) * update + (2.0 * ratio_next / half_width) * (residue / center_diag)
        ratio_prev = ratio_next
        result = result + update
    return result


def stencil_sweep(padded_adj, padded_stiff, adjoint, stiffness, load, support):
    shape = adjoint.shape
    diagonal = jnp.zeros(shape, jnp.float32)
    offsum = jnp.zeros(shape, jnp.float32)
    for shift_z in (-1, 0, 1):
        for shift_y in (-1, 0, 1):
            for shift_x in (-1, 0, 1):
                nonzero = abs(shift_z) + abs(shift_y) + abs(shift_x)
                if nonzero == 0:
                    continue
                weight = {1: 1.0, 2: 0.5, 3: 0.25}[nonzero]
                near_adj = padded_adj[1 + shift_z:1 + shift_z + shape[0], 1 + shift_y:1 + shift_y + shape[1], 1 + shift_x:1 + shift_x + shape[2]]
                near_stiff = padded_stiff[1 + shift_z:1 + shift_z + shape[0], 1 + shift_y:1 + shift_y + shape[1], 1 + shift_x:1 + shift_x + shape[2]]
                coupling = weight * 0.5 * (stiffness + near_stiff)
                diagonal = diagonal + coupling
                offsum = offsum + coupling * near_adj
    applied = diagonal * adjoint - offsum
    updated = adjoint + relax_omega * (load - applied) / diagonal
    return jnp.where(support, 0.0, updated)


def reference(sensitivity, density, load, adjoint, labels):
    design = labels == 0
    smoothed = chebyshev(sensitivity)
    filtered = jnp.where(design, smoothed, 0.0)
    cells = float(NZ * NY * NX)
    volume = jnp.sum(jnp.where(design, density, 0.0))
    magnitude = jnp.sum(jnp.abs(filtered))
    update_direction = jnp.where(design, filtered / (magnitude / cells + epsilon) - volume_penalty * (volume / cells - volume_target), 0.0)
    stiffness = stiff_floor + (1.0 - stiff_floor) * density ** 3
    adjoint_next = stencil_sweep(jnp.pad(adjoint, 1), jnp.pad(stiffness, 1), adjoint, stiffness, load, labels == 2)
    return update_direction, adjoint_next
```

```python
import functools

import numpy as np
import jax
import jax.numpy as jnp
from jax import lax
from jax.experimental import pallas as pl
from jax.experimental.pallas import tpu as pltpu
from jax.sharding import PartitionSpec as P

ITERS = 4
filter_weight = 8.0
stiff_floor = 0.05
relax_omega = 0.6
volume_target = 0.15
volume_penalty = 20.0
epsilon = 1e-06
center_diag = 1.0 + 6.0 * filter_weight
lower_eig = 1.0 / center_diag
upper_eig = (1.0 + 12.0 * filter_weight) / center_diag
middle_eig = (upper_eig + lower_eig) / 2.0
half_width = (upper_eig - lower_eig) / 2.0
sigma_ratio = middle_eig / half_width

MESH = pl.DeviceIdType.MESH
F32 = jnp.float32

CZ, CY, NX = 8, 64, 512
GZ, GY = 128, 2
GROUP = 16
ROWS = CY + 24
DEEP = ITERS
FZ = CZ + 2 * DEEP


def filter_coefficients():
    times_t = np.polynomial.chebyshev.chebmulx
    residue = np.zeros(ITERS + 2)
    residue[0] = 1.0

    def pad(series):
        return np.pad(series, (0, max(0, ITERS + 2 - len(series))))[: ITERS + 2]

    def apply(series):
        return center_diag * (middle_eig * series + half_width * pad(times_t(series)))

    update = residue / (center_diag * middle_eig)
    result = update.copy()
    ratio_prev = 1.0 / sigma_ratio
    for _ in range(ITERS):
        residue = residue - apply(update)
        ratio_next = 1.0 / (2.0 * sigma_ratio - ratio_prev)
        update = ratio_next * ratio_prev * update + 2.0 * ratio_next / half_width * (
            residue / center_diag
        )
        ratio_prev = ratio_next
        result = result + update
    return [float(value) for value in result[: ITERS + 1]]


GAMMA = filter_coefficients()
SELF = (1.0 - middle_eig) / half_width
NEAR = filter_weight / (center_diag * half_width)


def lane_edge(width, at):
    return lax.broadcasted_iota(jnp.int32, (width, 128), 1) == at


def shift_lanes(value):
    rows = value.shape[0]
    left = pltpu.roll(value, 1, 1)
    right = pltpu.roll(value, NX - 1, 1)
    first = jnp.where(lane_edge(rows, 0), 0.0, left[:, :128])
    last = jnp.where(lane_edge(rows, 127), 0.0, right[:, NX - 128 :])
    left = jnp.concatenate([first, left[:, 128:]], axis=1)
    right = jnp.concatenate([right[:, : NX - 128], last], axis=1)
    return left, right


def load_rows(ref, plane, start, rows):
    wide = ref[plane, pl.ds(start - 8, rows + 16), :]
    above = pltpu.roll(wide, 1, 0)[8 : 8 + rows]
    below = pltpu.roll(wide, rows + 15, 0)[8 : 8 + rows]
    return wide[8 : 8 + rows], above, below


def near_sum(ref, plane, start, rows):
    middle, above, below = load_rows(ref, plane, start, rows)
    left, right = shift_lanes(middle)
    over = ref[plane - 1, pl.ds(start, rows), :] + ref[plane + 1, pl.ds(start, rows), :]
    return middle, over + (above + below) + (left + right)


def main_kernel(
    sens, dens, load, adj, labels,
    filt_out, adj_out, lab_out, tot_out,
    e, b3, b2, b1, ud, stiff, prod, line, load_v, mine, got,
    in_sem, lo_send, lo_recv, hi_send, hi_recv, side_send, side_recv, ud_send, ud_recv, ar_send, ar_recv,
):
    z = lax.axis_index("gz")
    y = lax.axis_index("gy")
    up = (lax.rem(z + 1, GZ), y)
    down = (lax.rem(z + GZ - 1, GZ), y)
    side = (z, 1 - y)
    side_up = (up[0], 1 - y)
    side_down = (down[0], 1 - y)
    block = z // GROUP
    rank = lax.rem(z, GROUP)
    plane_rank = block * GY + y
    groups = ([], [])
    for d in range(1, GROUP):
        groups[0].append((block * GROUP + lax.rem(rank + d, GROUP), y))
        other = lax.rem(plane_rank + d, GROUP)
        groups[1].append(((other // GY) * GROUP + rank, lax.rem(other, GY)))

    partner = pl.ds(pl.multiple_of(72 - 64 * y, 8), 8)
    e[:, partner, :] = jnp.zeros((FZ, 8, NX), F32)
    ud[:, :, partner, :] = jnp.zeros((2, CZ + 2, 8, NX), F32)

    barrier = pltpu.get_barrier_semaphore()
    greeted = [up, down, side, side_up, side_down] + groups[0] + groups[1]
    for device in greeted:
        pl.semaphore_signal(barrier, inc=1, device_id=device, device_id_type=MESH)

    own = pl.multiple_of(8 + 8 * y, 8)
    mine_rows = pl.ds(own, CY)
    loads = [
        pltpu.make_async_copy(sens, e.at[pl.ds(DEEP, CZ), mine_rows, :], in_sem.at[0]),
        pltpu.make_async_copy(labels, lab_out, in_sem.at[1]),
        pltpu.make_async_copy(dens, ud.at[1, pl.ds(1, CZ), mine_rows, :], in_sem.at[2]),
        pltpu.make_async_copy(adj, ud.at[0, pl.ds(1, CZ), mine_rows, :], in_sem.at[3]),
        pltpu.make_async_copy(load, load_v, in_sem.at[4]),
    ]
    for copy in loads:
        copy.start()

    def clear(plane, _):
        zero = jnp.zeros((8, NX), F32)
        for ref in (e, b3, b2, b1):
            ref[plane, 0:8, :] = zero
            ref[plane, 80:88, :] = zero
        return 0

    lax.fori_loop(0, FZ, clear, 0)

    def clear_two(plane, _):
        zero = jnp.zeros((8, NX), F32)
        for ref in (ud.at[0], stiff, prod):
            ref[plane, 0:8, :] = zero
            ref[plane, 80:88, :] = zero
        return 0

    lax.fori_loop(0, CZ + 2, clear_two, 0)

    four_from = 68 - 52 * y
    four_to = 12 + 60 * y
    four_src = pl.ds(four_from, DEEP)
    four_dst = pl.ds(four_to, DEEP)

    def remote(src, dst, send, recv, device):
        return pltpu.make_async_remote_copy(src, dst, send, recv, device_id=device, device_id_type=MESH)

    side_copies = [
        remote(e.at[pl.ds(4, 8), four_src, :], e.at[pl.ds(4, 8), four_dst, :], side_send.at[0], side_recv.at[0], side),
        remote(e.at[pl.ds(8, 4), four_src, :], e.at[pl.ds(0, 4), four_dst, :], side_send.at[1], side_recv.at[1], side_up),
        remote(e.at[pl.ds(4, 4), four_src, :], e.at[pl.ds(12, 4), four_dst, :], side_send.at[2], side_recv.at[2], side_down),
    ]
    up_copies, down_copies = [], []
    for d in range(1, DEEP + 1):
        to_up, to_down = DEEP - d, DEEP + CZ - 1 + d
        up_copies.append(
            remote(e.at[to_up + CZ, mine_rows, :], e.at[to_up, mine_rows, :], lo_send.at[d - 1], lo_recv.at[d - 1], up)
        )
        down_copies.append(
            remote(e.at[to_down - CZ, mine_rows, :], e.at[to_down, mine_rows, :], hi_send.at[d - 1], hi_recv.at[d - 1], down)
        )

    one_from = 71 - 55 * y
    one_to = 15 + 57 * y
    one_src = pl.ds(one_from, 1)
    one_dst = pl.ds(one_to, 1)
    both = pl.ds(0, 2)
    ud_copies = [
        remote(ud.at[both, CZ, mine_rows, :], ud.at[both, 0, mine_rows, :], ud_send.at[0], ud_recv.at[0], up),
        remote(ud.at[both, 1, mine_rows, :], ud.at[both, CZ + 1, mine_rows, :], ud_send.at[1], ud_recv.at[1], down),
        remote(ud.at[both, pl.ds(1, CZ), one_src, :], ud.at[both, pl.ds(1, CZ), one_dst, :], ud_send.at[2], ud_recv.at[2], side),
        remote(ud.at[both, CZ, one_src, :], ud.at[both, 0, one_dst, :], ud_send.at[3], ud_recv.at[3], side_up),
        remote(ud.at[both, 1, one_src, :], ud.at[both, CZ + 1, one_dst, :], ud_send.at[4], ud_recv.at[4], side_down),
    ]

    loads[0].wait()
    pl.semaphore_wait(barrier, len(greeted))
    for d in range(DEEP):
        up_copies[d].start()
        down_copies[d].start()
        if d == 0:
            for copy in side_copies:
                copy.start()

    loads[1].wait()
    loads[2].wait()

    def volume_plane(plane, total):
        value = jnp.where(lab_out[plane] == 0, ud[1, plane + 1, mine_rows, :], 0.0)
        return total + jnp.sum(value.reshape(CY // 8, 8, NX), axis=0)

    volume = lax.fori_loop(0, CZ, volume_plane, jnp.zeros((8, NX), F32))
    loads[3].wait()
    loads[4].wait()

    def level3(plane, keep):
        for start in (8, 32, 56):
            middle, near = near_sum(e, plane, start, 24)
            value = (GAMMA[3] + 2.0 * SELF * GAMMA[4]) * middle - (2.0 * NEAR * GAMMA[4]) * near
            b3[plane, pl.ds(start, 24), :] = value * keep

    def level2(plane, keep):
        for start in (8, 32, 56):
            middle, near = near_sum(b3, plane, start, 24)
            value = (GAMMA[2] - GAMMA[4]) * e[plane, pl.ds(start, 24), :] - (2.0 * NEAR) * near
            if SELF != 0.0:
                value = value + (2.0 * SELF) * middle
            b2[plane, pl.ds(start, 24), :] = value * keep

    def level1(plane, keep):
        for start in (8, 32, 56):
            middle, near = near_sum(b2, plane, start, 24)
            value = GAMMA[1] * e[plane, pl.ds(start, 24), :] - b3[plane, pl.ds(start, 24), :] - (2.0 * NEAR) * near
            if SELF != 0.0:
                value = value + (2.0 * SELF) * middle
            b1[plane, pl.ds(start, 24), :] = value * keep

    def level0(plane, total):
        for part in range(CY // 16):
            start = pl.multiple_of(own + 16 * part, 8)
            rows = pl.ds(start, 16)
            middle, near = near_sum(b1, plane, start, 16)
            value = GAMMA[0] * e[plane, rows, :] - b2[plane, rows, :] - NEAR * near
            if SELF != 0.0:
                value = value + SELF * middle
            value = jnp.where(lab_out[plane - DEEP, 16 * part : 16 * part + 16, :] == 0, value, 0.0)
            filt_out[plane - DEEP, 16 * part : 16 * part + 16, :] = value
            size = jnp.abs(value)
            total = total + (size[:8] + size[8:])
        return total

    def keep_of(plane):
        outside = ((plane < DEEP) & (z == 0)) | ((plane >= DEEP + CZ) & (z == GZ - 1))
        return jnp.where(outside, 0.0, 1.0).astype(F32)

    def repeat(level, first, last):
        def body(plane, _):
            level(plane, 1.0)
            return 0

        lax.fori_loop(first, last, body, 0)

    side_copies[0].wait_recv()
    repeat(level3, 5, 11)
    repeat(level2, 6, 10)
    repeat(level1, 7, 9)
    side_copies[1].wait_recv()
    side_copies[2].wait_recv()

    total = jnp.zeros((8, NX), F32)
    for d in range(1, DEEP + 1):
        up_copies[d - 1].wait_recv()
        down_copies[d - 1].wait_recv()
        if d == 3:
            for copy in ud_copies:
                copy.start()

        @pl.when(z == 0)
        def _():
            e[DEEP - d] = jnp.zeros((ROWS, NX), F32)

        @pl.when(z == GZ - 1)
        def _():
            e[DEEP + CZ - 1 + d] = jnp.zeros((ROWS, NX), F32)

        def wave(at, total):
            def plane_of(low):
                return low + at * (FZ - 1 - 2 * low)

            level3(plane_of(5 - d), keep_of(plane_of(5 - d)))
            level2(plane_of(6 - d), keep_of(plane_of(6 - d)))
            level1(plane_of(7 - d), keep_of(plane_of(7 - d)))
            return level0(plane_of(8 - d), total)

        total = lax.fori_loop(0, 2, wave, total)

    def fold(value):
        lanes = value[:, :128] + value[:, 128:256] + value[:, 256:384] + value[:, 384:]
        return jnp.sum(lanes, axis=0, keepdims=True)

    row = lax.broadcasted_iota(jnp.int32, (8, 128), 0)
    mine[0] = jnp.where(row < 4, fold(total), fold(volume))

    def spread(phase):
        for d in range(GROUP - 1):
            remote(mine.at[phase], got.at[phase, d], ar_send.at[phase], ar_recv.at[phase], groups[phase][d]).start()

    def gather(phase):
        pltpu.make_async_copy(got.at[phase], got.at[phase], ar_recv.at[phase]).wait()
        return mine[phase] + jnp.sum(got[phase], axis=0)

    spread(0)

    for copy in ud_copies:
        copy.wait_recv()

    def sweep_lines(plane, _):
        outside = ((plane == 0) & (z == 0)) | ((plane == CZ + 1) & (z == GZ - 1))
        keep = jnp.where(outside, 0.0, 1.0).astype(F32)
        for start in (8, 32, 56):
            rows = pl.ds(start, 24)
            density = ud[1, plane, rows, :]
            field = ud[0, plane, rows, :] * keep
            value = (stiff_floor + (1.0 - stiff_floor) * (density * density * density)) * keep
            stiff[plane, rows, :] = value
            prod[plane, rows, :] = value * field
            ud[0, plane, rows, :] = field
        for part in range(CY // 16):
            start = pl.multiple_of(own + 16 * part, 8)
            for slot, ref in enumerate((stiff, ud.at[0], prod)):
                middle, above, below = load_rows(ref, plane, start, 16)
                value = middle + 0.5 * (above + below)
                left, right = shift_lanes(value)
                line[slot, plane, 16 * part : 16 * part + 16, :] = value + 0.5 * (left + right)
        return 0

    for copy in ud_copies:
        copy.wait_send()
    lax.fori_loop(0, CZ + 2, sweep_lines, 0)

    mine[1] = gather(0)
    spread(1)

    def sweep_out(plane, _):
        for part in range(CY // 16):
            here = slice(16 * part, 16 * part + 16)
            rows = pl.ds(pl.multiple_of(own + 16 * part, 8), 16)

            def stack(slot):
                return line[slot, plane + 1, here, :] + 0.5 * (
                    line[slot, plane, here, :] + line[slot, plane + 2, here, :]
                )

            value = stiff[plane + 1, rows, :]
            field = ud[0, plane + 1, rows, :]
            diagonal = 6.0 * value + stack(0)
            offsum = value * stack(1) + (stack(2) - 2.0 * prod[plane + 1, rows, :])
            applied = diagonal * field - offsum
            updated = field + relax_omega * (load_v[plane, here, :] - applied) / diagonal
            adj_out[plane, here, :] = jnp.where(lab_out[plane, here, :] == 2, 0.0, updated)
        return 0

    lax.fori_loop(0, CZ, sweep_out, 0)

    tot_out[...] = gather(1)
    for phase in range(2):
        pltpu.make_async_copy(got.at[phase], got.at[phase], ar_send.at[phase]).wait()
    for copy in side_copies + up_copies + down_copies:
        copy.wait_send()


def last_kernel(filt, adj_in, labels, tot, dir_out, adj_out, held, sem):
    whole = pltpu.make_async_copy(adj_in, adj_out, sem.at[CZ])
    whole.start()
    cells = float(GZ * CZ * GY * CY * NX)
    magnitude = jnp.sum(tot[0:1, :], axis=1, keepdims=True)
    volume = jnp.sum(tot[4:5, :], axis=1, keepdims=True)
    scale = 1.0 / (magnitude / cells + epsilon)
    offset = volume_penalty * (volume / cells - volume_target)
    scale = jnp.broadcast_to(scale, (CY, NX))
    offset = jnp.broadcast_to(offset, (CY, NX))
    copies = []
    for plane in range(CZ):
        held[plane] = jnp.where(labels[plane] == 0, filt[plane] * scale - offset, 0.0)
        copy = pltpu.make_async_copy(held.at[plane], dir_out.at[plane], sem.at[plane])
        copy.start()
        copies.append(copy)
    for copy in copies + [whole]:
        copy.wait()


def on_device(sensitivity, density, load, adjoint, labels):
    shape = (CZ, CY, NX)
    dma = pltpu.SemaphoreType.DMA
    vmem = pl.BlockSpec(memory_space=pltpu.VMEM)
    hbm = pl.BlockSpec(memory_space=pltpu.HBM)
    filtered, swept, held_labels, totals = pl.pallas_call(
        main_kernel,
        out_shape=(
            jax.ShapeDtypeStruct(shape, F32),
            jax.ShapeDtypeStruct(shape, F32),
            jax.ShapeDtypeStruct(shape, jnp.int32),
            jax.ShapeDtypeStruct((8, 128), F32),
        ),
        in_specs=[hbm] * 5,
        out_specs=(vmem,) * 4,
        scratch_shapes=[
            pltpu.VMEM((FZ, ROWS, NX), F32),
            pltpu.VMEM((FZ, ROWS, NX), F32),
            pltpu.VMEM((FZ, ROWS, NX), F32),
            pltpu.VMEM((FZ, ROWS, NX), F32),
            pltpu.VMEM((2, CZ + 2, ROWS, NX), F32),
            pltpu.VMEM((CZ + 2, ROWS, NX), F32),
            pltpu.VMEM((CZ + 2, ROWS, NX), F32),
            pltpu.VMEM((3, CZ + 2, CY, NX), F32),
            pltpu.VMEM(shape, F32),
            pltpu.VMEM((2, 8, 128), F32),
            pltpu.VMEM((2, GROUP - 1, 8, 128), F32),
            dma((5,)),
            dma((DEEP,)),
            dma((DEEP,)),
            dma((DEEP,)),
            dma((DEEP,)),
            dma((3,)),
            dma((3,)),
            dma((5,)),
            dma((5,)),
            dma((2,)),
            dma((2,)),
        ],
        compiler_params=pltpu.CompilerParams(
            collective_id=1, has_side_effects=True, vmem_limit_bytes=40 * 2**20
        ),
        name="filter_and_sweep",
    )(sensitivity, density, load, adjoint, labels)
    return pl.pallas_call(
        last_kernel,
        out_shape=(jax.ShapeDtypeStruct(shape, F32), jax.ShapeDtypeStruct(shape, F32)),
        in_specs=[vmem] * 4,
        out_specs=(hbm, hbm),
        scratch_shapes=[pltpu.VMEM(shape, F32), dma((CZ + 1,))],
        name="normalise_and_store",
    )(filtered, swept, held_labels, totals)


def solution(mesh):
    placed = (P("gz", "gy", None),) * 5
    return jax.shard_map(
        on_device,
        mesh=mesh,
        in_specs=placed,
        out_specs=(P("gz", "gy", None), P("gz", "gy", None)),
        check_vma=False,
    )
```

```python
import functools

import numpy as np
import jax
import jax.numpy as jnp
from jax import lax
from jax.experimental import pallas as pl
from jax.experimental.pallas import tpu as pltpu
from jax.sharding import PartitionSpec as P

ITERS = 4
filter_weight = 8.0
stiff_floor = 0.05
relax_omega = 0.6
volume_target = 0.15
volume_penalty = 20.0
epsilon = 1e-06
center_diag = 1.0 + 6.0 * filter_weight
lower_eig = 1.0 / center_diag
upper_eig = (1.0 + 12.0 * filter_weight) / center_diag
middle_eig = (upper_eig + lower_eig) / 2.0
half_width = (upper_eig - lower_eig) / 2.0
sigma_ratio = middle_eig / half_width

MESH = pl.DeviceIdType.MESH
F32 = jnp.float32

CZ, CY, NX = 8, 64, 512
GZ, GY = 128, 2
GROUP = 16
ROWS = CY + 24
DEEP = ITERS
FZ = CZ + 2 * DEEP


def filter_coefficients():
    times_t = np.polynomial.chebyshev.chebmulx
    residue = np.zeros(ITERS + 2)
    residue[0] = 1.0

    def pad(series):
        return np.pad(series, (0, max(0, ITERS + 2 - len(series))))[: ITERS + 2]

    def apply(series):
        return center_diag * (middle_eig * series + half_width * pad(times_t(series)))

    update = residue / (center_diag * middle_eig)
    result = update.copy()
    ratio_prev = 1.0 / sigma_ratio
    for _ in range(ITERS):
        residue = residue - apply(update)
        ratio_next = 1.0 / (2.0 * sigma_ratio - ratio_prev)
        update = ratio_next * ratio_prev * update + 2.0 * ratio_next / half_width * (
            residue / center_diag
        )
        ratio_prev = ratio_next
        result = result + update
    return [float(value) for value in result[: ITERS + 1]]


GAMMA = filter_coefficients()
SELF = (1.0 - middle_eig) / half_width
NEAR = filter_weight / (center_diag * half_width)
TILES = NX // 128


def sine_basis():
    index = np.arange(1, NX + 1, dtype=np.float64)
    basis = np.sqrt(2.0 / (NX + 1)) * np.sin(np.pi * np.outer(index, index) / (NX + 1))
    high = basis.astype(jnp.bfloat16)
    low = (basis - high.astype(np.float64)).astype(jnp.bfloat16)
    along = 2.0 * np.cos(np.pi * index / (NX + 1))
    factors = np.zeros((8, NX))
    factors[0] = GAMMA[3] + 2.0 * GAMMA[4] * (SELF - NEAR * along)
    factors[1] = 2.0 * (SELF - NEAR * along)
    factors[2] = SELF - NEAR * along
    return np.stack([high, low]), factors.astype(np.float32)


BASIS, FACTORS = sine_basis()


def transform(value, basis):
    high = value.astype(jnp.bfloat16)
    low = (value - high.astype(F32)).astype(jnp.bfloat16)
    first = jnp.dot(high, basis[0], preferred_element_type=F32)
    second = jnp.dot(low, basis[0], preferred_element_type=F32)
    third = jnp.dot(high, basis[1], preferred_element_type=F32)
    return first + (second + third)


def smooth_lanes(tiles):
    lane = lax.broadcasted_iota(jnp.int32, tiles[0].shape, 1)
    from_left = [pltpu.roll(tile, 1, 1) for tile in tiles]
    from_right = [pltpu.roll(tile, 127, 1) for tile in tiles]
    out = []
    for j, tile in enumerate(tiles):
        left = jnp.where(lane == 0, from_left[j - 1] if j > 0 else 0.0, from_left[j])
        right = jnp.where(lane == 127, from_right[j + 1] if j + 1 < TILES else 0.0, from_right[j])
        out.append(tile + 0.5 * (left + right))
    return out


def main_kernel(
    sens, dens, load, adj, labels, basis_in, factors_in,
    filt_out, adj_out, lab_out, tot_out,
    raw, basis, factors, e, b3, b2, b1, flat, ud, stiff, smooth, column, load_v, mine, got,
    in_sem, lo_send, lo_recv, hi_send, hi_recv, side_send, side_recv, ud_send, ud_recv, ar_send, ar_recv,
):
    z = lax.axis_index("gz")
    y = lax.axis_index("gy")
    up = (lax.rem(z + 1, GZ), y)
    down = (lax.rem(z + GZ - 1, GZ), y)
    side = (z, 1 - y)
    side_up = (up[0], 1 - y)
    side_down = (down[0], 1 - y)
    block = z // GROUP
    rank = lax.rem(z, GROUP)
    plane_rank = block * GY + y
    groups = ([], [])
    for d in range(1, GROUP):
        groups[0].append((block * GROUP + lax.rem(rank + d, GROUP), y))
        other = lax.rem(plane_rank + d, GROUP)
        groups[1].append(((other // GY) * GROUP + rank, lax.rem(other, GY)))

    own = pl.multiple_of(8 + 8 * y, 8)
    mine_rows = pl.ds(own, CY)
    partner = pl.ds(pl.multiple_of(72 - 64 * y, 8), 8)
    all_tiles = pl.ds(0, TILES)
    loads = [
        pltpu.make_async_copy(sens, raw, in_sem.at[0]),
        pltpu.make_async_copy(basis_in, basis, in_sem.at[1]),
        pltpu.make_async_copy(factors_in, factors, in_sem.at[2]),
        pltpu.make_async_copy(labels, lab_out, in_sem.at[3]),
        pltpu.make_async_copy(load, load_v, in_sem.at[4]),
    ]
    for j in range(TILES):
        for slot, array in enumerate((adj, dens)):
            loads.append(
                pltpu.make_async_copy(
                    array.at[:, :, pl.ds(128 * j, 128)],
                    ud.at[slot, j, pl.ds(1, CZ), mine_rows, :],
                    in_sem.at[5 + 2 * j + slot],
                )
            )
    for copy in loads:
        copy.start()

    e[:, :, partner, :] = jnp.zeros((TILES, FZ, 8, 128), F32)
    ud[:, :, :, partner, :] = jnp.zeros((2, TILES, CZ + 2, 8, 128), F32)

    barrier = pltpu.get_barrier_semaphore()
    greeted = [up, down, side, side_up, side_down] + groups[0] + groups[1]
    for device in greeted:
        pl.semaphore_signal(barrier, inc=1, device_id=device, device_id_type=MESH)

    def clear(j, _):
        for ref in (e, b3, b2, b1):
            ref[j, :, 0:8, :] = jnp.zeros((FZ, 8, 128), F32)
            ref[j, :, 80:88, :] = jnp.zeros((FZ, 8, 128), F32)
        for slot in range(3):
            smooth[slot, j, :, 0:8, :] = jnp.zeros((CZ + 2, 8, 128), F32)
            smooth[slot, j, :, 80:88, :] = jnp.zeros((CZ + 2, 8, 128), F32)
            column[slot, j, 0:8, :] = jnp.zeros((8, 128), F32)
            column[slot, j, 80:88, :] = jnp.zeros((8, 128), F32)
        return 0

    lax.fori_loop(0, TILES, clear, 0)

    loads[0].wait()
    loads[1].wait()
    loads[2].wait()
    spectrum = transform(raw[...].reshape(CZ * CY, NX), basis)
    for plane in range(CZ):
        for j in range(TILES):
            e[j, DEEP + plane, mine_rows, :] = spectrum[CY * plane : CY * plane + CY, 128 * j : 128 * j + 128]

    four_src, four_dst = pl.ds(68 - 52 * y, 4), pl.ds(12 + 60 * y, 4)
    three_src, three_dst = pl.ds(69 - 53 * y, 3), pl.ds(13 + 59 * y, 3)

    def remote(src, dst, send, recv, device):
        return pltpu.make_async_remote_copy(src, dst, send, recv, device_id=device, device_id_type=MESH)

    def part(planes, rows):
        return e.at[all_tiles, planes, rows, :]

    side_copies = [
        remote(part(pl.ds(4, 8), four_src), part(pl.ds(4, 8), four_dst), side_send.at[0], side_recv.at[0], side),
        remote(part(pl.ds(9, 3), three_src), part(pl.ds(1, 3), three_dst), side_send.at[1], side_recv.at[1], side_up),
        remote(part(pl.ds(4, 3), three_src), part(pl.ds(12, 3), three_dst), side_send.at[2], side_recv.at[2], side_down),
    ]
    up_copies, down_copies = [], []
    for d in range(1, DEEP + 1):
        to_up, to_down = DEEP - d, DEEP + CZ - 1 + d
        up_copies.append(
            remote(part(to_up + CZ, mine_rows), part(to_up, mine_rows), lo_send.at[d - 1], lo_recv.at[d - 1], up)
        )
        down_copies.append(
            remote(part(to_down - CZ, mine_rows), part(to_down, mine_rows), hi_send.at[d - 1], hi_recv.at[d - 1], down)
        )

    one_src, one_dst = pl.ds(71 - 55 * y, 1), pl.ds(15 + 57 * y, 1)

    def ud_part(planes, rows):
        return ud.at[pl.ds(0, 2), all_tiles, planes, rows, :]

    inner = pl.ds(1, CZ)
    ud_copies = [
        remote(ud_part(CZ, mine_rows), ud_part(0, mine_rows), ud_send.at[0], ud_recv.at[0], up),
        remote(ud_part(1, mine_rows), ud_part(CZ + 1, mine_rows), ud_send.at[1], ud_recv.at[1], down),
        remote(ud_part(inner, one_src), ud_part(inner, one_dst), ud_send.at[2], ud_recv.at[2], side),
        remote(ud_part(CZ, one_src), ud_part(0, one_dst), ud_send.at[3], ud_recv.at[3], side_up),
        remote(ud_part(1, one_src), ud_part(CZ + 1, one_dst), ud_send.at[4], ud_recv.at[4], side_down),
    ]

    def sweep_lines(plane, rows, size, keep=None):
        fields = ([], [], [])
        for j in range(TILES):
            density = ud[1, j, plane, rows, :]
            field = ud[0, j, plane, rows, :]
            value = stiff_floor + (1.0 - stiff_floor) * (density * density * density)
            if keep is not None:
                value = value * keep
                field = field * keep
            fields[0].append(value)
            fields[1].append(field)
            fields[2].append(value * field)
        for slot in range(3):
            for j, tile in enumerate(smooth_lanes(fields[slot])):
                smooth[slot, j, plane, rows, :] = tile
        return fields[0]

    def sweep_own(plane, _):
        for k in range(CY // 16):
            rows = pl.ds(pl.multiple_of(own + 16 * k, 8), 16)
            for j, tile in enumerate(sweep_lines(plane, rows, 16)):
                stiff[j, plane, rows, :] = tile
        return 0

    def volume_plane(plane, total):
        for j in range(TILES):
            here = lab_out[plane, :, 128 * j : 128 * j + 128] == 0
            value = jnp.where(here, ud[1, j, plane + 1, mine_rows, :], 0.0)
            total = total + jnp.sum(value.reshape(CY // 8, 8, 128), axis=0)
        return total

    pl.semaphore_wait(barrier, len(greeted))
    for copy in (up_copies[0], down_copies[0]):
        copy.start()
    for copy in side_copies:
        copy.start()
    for copy in loads[3:]:
        copy.wait()
    volume = lax.fori_loop(0, CZ, volume_plane, jnp.zeros((8, 128), F32))
    for copy in (up_copies[0], down_copies[0]):
        copy.wait_send()
    for copy in (up_copies[1], down_copies[1]):
        copy.start()
    lax.fori_loop(1, 3, sweep_own, 0)
    for copy in (up_copies[1], down_copies[1]):
        copy.wait_send()
    for copy in (up_copies[2], down_copies[2]):
        copy.start()
    lax.fori_loop(3, 5, sweep_own, 0)
    for copy in (up_copies[2], down_copies[2]):
        copy.wait_send()
    for copy in (up_copies[3], down_copies[3]):
        copy.start()
    lax.fori_loop(5, 7, sweep_own, 0)
    for copy in ud_copies:
        copy.start()
    lax.fori_loop(7, CZ + 1, sweep_own, 0)

    def across(ref, j, plane, start, rows):
        over = ref[j, plane - 1, pl.ds(start, rows), :] + ref[j, plane + 1, pl.ds(start, rows), :]
        return over + (ref[j, plane, pl.ds(start - 1, rows), :] + ref[j, plane, pl.ds(start + 1, rows), :])

    def factor(row, j, rows):
        return jnp.broadcast_to(factors[row : row + 1, 128 * j : 128 * j + 128], (rows, 128))

    body = pl.ds(8, 72)

    def put(ref, j, plane, value, keep):
        ref[j, plane, body, :] = value if keep is None else value * keep

    def level3(plane, keep=None):
        for j in range(TILES):
            value = factor(0, j, 72) * e[j, plane, body, :] - (2.0 * NEAR * GAMMA[4]) * across(e, j, plane, 8, 72)
            put(b3, j, plane, value, keep)

    def level2(plane, keep=None):
        for j in range(TILES):
            value = (GAMMA[2] - GAMMA[4]) * e[j, plane, body, :] + factor(1, j, 72) * b3[j, plane, body, :]
            put(b2, j, plane, value - (2.0 * NEAR) * across(b3, j, plane, 8, 72), keep)

    def level1(plane, keep=None):
        for j in range(TILES):
            value = GAMMA[1] * e[j, plane, body, :] + factor(1, j, 72) * b2[j, plane, body, :]
            value = value - b3[j, plane, body, :]
            put(b1, j, plane, value - (2.0 * NEAR) * across(b2, j, plane, 8, 72), keep)

    def level0(plane, slot):
        for j in range(TILES):
            value = GAMMA[0] * e[j, plane, mine_rows, :] + factor(2, j, CY) * b1[j, plane, mine_rows, :]
            value = value - b2[j, plane, mine_rows, :]
            flat[slot, :, 128 * j : 128 * j + 128] = value - NEAR * across(b1, j, plane, own, CY)

    def repeat(level, first, last):
        def step(plane, _):
            level(plane)
            return 0

        lax.fori_loop(first, last, step, 0)

    side_copies[0].wait_recv()
    repeat(level3, 5, 11)
    repeat(level2, 6, 10)
    repeat(level1, 7, 9)
    side_copies[1].wait_recv()
    side_copies[2].wait_recv()

    low_keep = jnp.where(z == 0, 0.0, 1.0).astype(F32)
    high_keep = jnp.where(z == GZ - 1, 0.0, 1.0).astype(F32)

    def keep_of(plane):
        return low_keep if plane < DEEP else high_keep if plane >= DEEP + CZ else None

    def back(first, count, planes, total):
        value = transform(flat[first : first + count].reshape(count * CY, NX), basis)
        for k, plane in enumerate(planes):
            kept = jnp.where(lab_out[plane] == 0, value[CY * k : CY * k + CY], 0.0)
            filt_out[plane] = kept
            total = total + jnp.sum(jnp.abs(kept).reshape(CY // 8, 8, NX), axis=0)
        return total

    total = jnp.zeros((8, NX), F32)
    order = []
    for d in range(1, DEEP + 1):
        up_copies[d - 1].wait_recv()
        down_copies[d - 1].wait_recv()

        @pl.when(z == 0)
        def _():
            e[:, DEEP - d] = jnp.zeros((TILES, ROWS, 128), F32)

        @pl.when(z == GZ - 1)
        def _():
            e[:, DEEP + CZ - 1 + d] = jnp.zeros((TILES, ROWS, 128), F32)

        for level, low in ((level3, 5 - d), (level2, 6 - d), (level1, 7 - d)):
            for plane in (low, FZ - 1 - low):
                level(plane, keep_of(plane))
        for low in (8 - d, FZ - 1 - (8 - d)):
            level0(low, len(order))
            order.append(low - DEEP)
        if d == DEEP - 1:
            total = back(0, 6, order, total)
    total = back(6, 2, order[6:], total)

    def fold(value):
        return jnp.sum(value, axis=0, keepdims=True)

    row = lax.broadcasted_iota(jnp.int32, (8, 128), 0)
    size = total[:, :128] + total[:, 128:256] + total[:, 256:384] + total[:, 384:]
    mine[0] = jnp.where(row < 4, fold(size), fold(volume))

    def spread(phase):
        for d in range(GROUP - 1):
            remote(mine.at[phase], got.at[phase, d], ar_send.at[phase], ar_recv.at[phase], groups[phase][d]).start()

    def gather(phase):
        pltpu.make_async_copy(got.at[phase], got.at[phase], ar_recv.at[phase]).wait()
        return mine[phase] + jnp.sum(got[phase], axis=0)

    spread(0)

    for copy in ud_copies:
        copy.wait_recv()

    for plane, keep in ((0, low_keep), (CZ + 1, high_keep)):
        for k in range(3):
            sweep_lines(plane, pl.ds(8 + 24 * k, 24), 24, keep)

    def sweep_partner(plane, _):
        sweep_lines(plane, partner, 8)
        return 0

    lax.fori_loop(1, CZ + 1, sweep_partner, 0)

    def sweep_out(plane, _):
        for slot in range(3):
            for j in range(TILES):
                column[slot, j, body, :] = smooth[slot, j, plane + 1, body, :] + 0.5 * (
                    smooth[slot, j, plane, body, :] + smooth[slot, j, plane + 2, body, :]
                )
        for j in range(TILES):
            lanes = slice(128 * j, 128 * j + 128)

            def stack(slot):
                return column[slot, j, mine_rows, :] + 0.5 * (
                    column[slot, j, pl.ds(own - 1, CY), :] + column[slot, j, pl.ds(own + 1, CY), :]
                )

            value = stiff[j, plane + 1, mine_rows, :]
            field = ud[0, j, plane + 1, mine_rows, :]
            diagonal = 6.0 * value + stack(0)
            offsum = value * (stack(1) - 2.0 * field) + stack(2)
            applied = diagonal * field - offsum
            updated = field + relax_omega * (load_v[plane, :, lanes] - applied) / diagonal
            adj_out[plane, :, lanes] = jnp.where(lab_out[plane, :, lanes] == 2, 0.0, updated)
        return 0

    lax.fori_loop(0, CZ // 4, sweep_out, 0)

    mine[1] = gather(0)
    spread(1)

    lax.fori_loop(CZ // 4, CZ, sweep_out, 0)

    tot_out[...] = gather(1)
    for phase in range(2):
        pltpu.make_async_copy(got.at[phase], got.at[phase], ar_send.at[phase]).wait()
    for copy in side_copies + ud_copies + up_copies[3:] + down_copies[3:]:
        copy.wait_send()


def last_kernel(filt, adj_in, labels, tot, dir_out, adj_out, held, sem):
    whole = pltpu.make_async_copy(adj_in, adj_out, sem.at[CZ])
    whole.start()
    cells = float(GZ * CZ * GY * CY * NX)
    magnitude = jnp.sum(tot[0:1, :], axis=1, keepdims=True)
    volume = jnp.sum(tot[4:5, :], axis=1, keepdims=True)
    scale = 1.0 / (magnitude / cells + epsilon)
    offset = volume_penalty * (volume / cells - volume_target)
    scale = jnp.broadcast_to(scale, (CY, NX))
    offset = jnp.broadcast_to(offset, (CY, NX))
    copies = []
    for plane in range(CZ):
        held[plane] = jnp.where(labels[plane] == 0, filt[plane] * scale - offset, 0.0)
        copy = pltpu.make_async_copy(held.at[plane], dir_out.at[plane], sem.at[plane])
        copy.start()
        copies.append(copy)
    for copy in copies + [whole]:
        copy.wait()


def on_device(sensitivity, density, load, adjoint, labels):
    shape = (CZ, CY, NX)
    dma = pltpu.SemaphoreType.DMA
    vmem = pl.BlockSpec(memory_space=pltpu.VMEM)
    hbm = pl.BlockSpec(memory_space=pltpu.HBM)
    arrays = (sensitivity, density, load, adjoint, labels, jnp.asarray(BASIS), jnp.asarray(FACTORS))
    filtered, swept, held_labels, totals = pl.pallas_call(
        main_kernel,
        out_shape=(
            pltpu.VMEM(shape, F32),
            pltpu.VMEM(shape, F32),
            pltpu.VMEM(shape, jnp.int32),
            pltpu.VMEM((8, 128), F32),
        ),
        in_specs=[hbm] * 7,
        out_specs=(vmem,) * 4,
        scratch_shapes=[
            pltpu.VMEM(shape, F32),
            pltpu.VMEM((2, NX, NX), jnp.bfloat16),
            pltpu.VMEM((8, NX), F32),
            pltpu.VMEM((TILES, FZ, ROWS, 128), F32),
            pltpu.VMEM((TILES, FZ, ROWS, 128), F32),
            pltpu.VMEM((TILES, FZ, ROWS, 128), F32),
            pltpu.VMEM((TILES, FZ, ROWS, 128), F32),
            pltpu.VMEM(shape, F32),
            pltpu.VMEM((2, TILES, CZ + 2, ROWS, 128), F32),
            pltpu.VMEM((TILES, CZ + 2, ROWS, 128), F32),
            pltpu.VMEM((3, TILES, CZ + 2, ROWS, 128), F32),
            pltpu.VMEM((3, TILES, ROWS, 128), F32),
            pltpu.VMEM(shape, F32),
            pltpu.VMEM((2, 8, 128), F32),
            pltpu.VMEM((2, GROUP - 1, 8, 128), F32),
            dma((5 + 2 * TILES,)),
            dma((DEEP,)),
            dma((DEEP,)),
            dma((DEEP,)),
            dma((DEEP,)),
            dma((3,)),
            dma((3,)),
            dma((5,)),
            dma((5,)),
            dma((2,)),
            dma((2,)),
        ],
        compiler_params=pltpu.CompilerParams(
            collective_id=1, has_side_effects=True, vmem_limit_bytes=40 * 2**20
        ),
        name="filter_and_sweep",
    )(*[pltpu.with_memory_space_constraint(array, pltpu.HBM) for array in arrays])
    filtered, swept, held_labels, totals = (
        pltpu.with_memory_space_constraint(array, pltpu.VMEM) for array in (filtered, swept, held_labels, totals)
    )
    return pl.pallas_call(
        last_kernel,
        out_shape=(jax.ShapeDtypeStruct(shape, F32), jax.ShapeDtypeStruct(shape, F32)),
        in_specs=[vmem] * 4,
        out_specs=(hbm, hbm),
        scratch_shapes=[pltpu.VMEM(shape, F32), dma((CZ + 1,))],
        name="normalise_and_store",
    )(filtered, swept, held_labels, totals)


def solution(mesh):
    placed = (P("gz", "gy", None),) * 5
    return jax.shard_map(
        on_device,
        mesh=mesh,
        in_specs=placed,
        out_specs=(P("gz", "gy", None), P("gz", "gy", None)),
        check_vma=False,
    )
```

```python
import functools

import numpy as np
import jax
import jax.numpy as jnp
from jax import lax
from jax.experimental import pallas as pl
from jax.experimental.pallas import tpu as pltpu
from jax.sharding import PartitionSpec as P

ITERS = 4
filter_weight = 8.0
stiff_floor = 0.05
relax_omega = 0.6
volume_target = 0.15
volume_penalty = 20.0
epsilon = 1e-06
center_diag = 1.0 + 6.0 * filter_weight
lower_eig = 1.0 / center_diag
upper_eig = (1.0 + 12.0 * filter_weight) / center_diag
middle_eig = (upper_eig + lower_eig) / 2.0
half_width = (upper_eig - lower_eig) / 2.0
sigma_ratio = middle_eig / half_width

MESH = pl.DeviceIdType.MESH
F32 = jnp.float32

CZ, CY, NX = 8, 64, 512
GZ, GY = 128, 2
GROUP = 16
ROWS = CY + 24
DEEP = ITERS
FZ = CZ + 2 * DEEP
PIECES = (2, 1, 1)
FIRSTS = {1: 0, 3: 1, 4: 2}


def filter_coefficients():
    times_t = np.polynomial.chebyshev.chebmulx
    residue = np.zeros(ITERS + 2)
    residue[0] = 1.0

    def pad(series):
        return np.pad(series, (0, max(0, ITERS + 2 - len(series))))[: ITERS + 2]

    def apply(series):
        return center_diag * (middle_eig * series + half_width * pad(times_t(series)))

    update = residue / (center_diag * middle_eig)
    result = update.copy()
    ratio_prev = 1.0 / sigma_ratio
    for _ in range(ITERS):
        residue = residue - apply(update)
        ratio_next = 1.0 / (2.0 * sigma_ratio - ratio_prev)
        update = ratio_next * ratio_prev * update + 2.0 * ratio_next / half_width * (
            residue / center_diag
        )
        ratio_prev = ratio_next
        result = result + update
    return [float(value) for value in result[: ITERS + 1]]


GAMMA = filter_coefficients()
SELF = (1.0 - middle_eig) / half_width
NEAR = filter_weight / (center_diag * half_width)
TILES = NX // 128


def sine_basis():
    index = np.arange(1, NX + 1, dtype=np.float64)
    basis = np.sqrt(2.0 / (NX + 1)) * np.sin(np.pi * np.outer(index, index) / (NX + 1))
    high = basis.astype(jnp.bfloat16)
    low = (basis - high.astype(np.float64)).astype(jnp.bfloat16)
    along = 2.0 * np.cos(np.pi * index / (NX + 1))
    factors = np.zeros((8, NX))
    factors[0] = GAMMA[3] + 2.0 * GAMMA[4] * (SELF - NEAR * along)
    factors[1] = 2.0 * (SELF - NEAR * along)
    factors[2] = SELF - NEAR * along
    return np.stack([high, low]), factors.astype(np.float32)


BASIS, FACTORS = sine_basis()


def transform(value, basis):
    high = value.astype(jnp.bfloat16)
    low = (value - high.astype(F32)).astype(jnp.bfloat16)
    first = jnp.dot(high, basis[0], preferred_element_type=F32)
    second = jnp.dot(low, basis[0], preferred_element_type=F32)
    third = jnp.dot(high, basis[1], preferred_element_type=F32)
    return first + (second + third)


def smooth_lanes(tiles):
    lane = lax.broadcasted_iota(jnp.int32, tiles[0].shape, 1)
    from_left = [pltpu.roll(tile, 1, 1) for tile in tiles]
    from_right = [pltpu.roll(tile, 127, 1) for tile in tiles]
    out = []
    for j, tile in enumerate(tiles):
        left = jnp.where(lane == 0, from_left[j - 1] if j > 0 else 0.0, from_left[j])
        right = jnp.where(lane == 127, from_right[j + 1] if j + 1 < TILES else 0.0, from_right[j])
        out.append(tile + 0.5 * (left + right))
    return out


def main_kernel(
    sens, dens, load, adj, labels, basis_in, factors_in,
    filt_out, adj_out, lab_out, tot_out,
    raw, basis, factors, e, b3, b2, b1, flat, ud, stiff, smooth, column, load_v, mine, got,
    in_sem, lo_send, lo_recv, hi_send, hi_recv, side_send, side_recv, ud_send, ud_recv, ar_send, ar_recv,
):
    z = lax.axis_index("gz")
    y = lax.axis_index("gy")
    up = (lax.rem(z + 1, GZ), y)
    down = (lax.rem(z + GZ - 1, GZ), y)
    side = (z, 1 - y)
    side_up = (up[0], 1 - y)
    side_down = (down[0], 1 - y)
    block = z // GROUP
    rank = lax.rem(z, GROUP)
    plane_rank = block * GY + y
    groups = ([], [])
    for d in range(1, GROUP):
        groups[0].append((block * GROUP + lax.rem(rank + d, GROUP), y))
        other = lax.rem(plane_rank + d, GROUP)
        groups[1].append(((other // GY) * GROUP + rank, lax.rem(other, GY)))

    own = pl.multiple_of(8 + 8 * y, 8)
    mine_rows = pl.ds(own, CY)
    partner = pl.ds(pl.multiple_of(72 - 64 * y, 8), 8)
    all_tiles = pl.ds(0, TILES)
    loads = [
        pltpu.make_async_copy(sens, raw, in_sem.at[0]),
        pltpu.make_async_copy(basis_in, basis, in_sem.at[1]),
        pltpu.make_async_copy(factors_in, factors, in_sem.at[2]),
        pltpu.make_async_copy(labels, lab_out, in_sem.at[3]),
        pltpu.make_async_copy(load, load_v, in_sem.at[4]),
    ]
    for j in range(TILES):
        for slot, array in enumerate((adj, dens)):
            loads.append(
                pltpu.make_async_copy(
                    array.at[:, :, pl.ds(128 * j, 128)],
                    ud.at[slot, j, pl.ds(1, CZ), mine_rows, :],
                    in_sem.at[5 + 2 * j + slot],
                )
            )
    for copy in loads[:3]:
        copy.start()

    e[:, :, partner, :] = jnp.zeros((TILES, FZ, 8, 128), F32)
    ud[:, :, :, partner, :] = jnp.zeros((2, TILES, CZ + 2, 8, 128), F32)

    barrier = pltpu.get_barrier_semaphore()
    greeted = [up, down, side, side_up, side_down] + groups[0] + groups[1]
    for device in greeted:
        pl.semaphore_signal(barrier, inc=1, device_id=device, device_id_type=MESH)
    for copy in loads[3:]:
        copy.start()

    def clear(j, _):
        for ref in (e, b3, b2, b1):
            ref[j, :, 0:8, :] = jnp.zeros((FZ, 8, 128), F32)
            ref[j, :, 80:88, :] = jnp.zeros((FZ, 8, 128), F32)
        for slot in range(3):
            smooth[slot, j, :, 0:8, :] = jnp.zeros((CZ + 2, 8, 128), F32)
            smooth[slot, j, :, 80:88, :] = jnp.zeros((CZ + 2, 8, 128), F32)
            column[slot, j, 0:8, :] = jnp.zeros((8, 128), F32)
            column[slot, j, 80:88, :] = jnp.zeros((8, 128), F32)
        return 0

    lax.fori_loop(0, TILES, clear, 0)

    loads[0].wait()
    loads[1].wait()
    loads[2].wait()
    spectrum = transform(raw[...].reshape(CZ * CY, NX), basis)
    for plane in range(CZ):
        for j in range(TILES):
            e[j, DEEP + plane, mine_rows, :] = spectrum[CY * plane : CY * plane + CY, 128 * j : 128 * j + 128]

    four_src, four_dst = pl.ds(68 - 52 * y, 4), pl.ds(12 + 60 * y, 4)
    three_src, three_dst = pl.ds(69 - 53 * y, 3), pl.ds(13 + 59 * y, 3)

    def remote(src, dst, send, recv, device):
        return pltpu.make_async_remote_copy(src, dst, send, recv, device_id=device, device_id_type=MESH)

    def part(planes, rows):
        return e.at[all_tiles, planes, rows, :]

    side_copies = [
        remote(part(pl.ds(4, 8), four_src), part(pl.ds(4, 8), four_dst), side_send.at[0], side_recv.at[0], side),
        remote(part(pl.ds(9, 3), three_src), part(pl.ds(1, 3), three_dst), side_send.at[1], side_recv.at[1], side_up),
        remote(part(pl.ds(4, 3), three_src), part(pl.ds(12, 3), three_dst), side_send.at[2], side_recv.at[2], side_down),
    ]
    up_copies, down_copies = [], []
    near = 0
    for at, count in enumerate(PIECES):
        low, high = pl.ds(DEEP - near - count, count), pl.ds(DEEP + CZ + near, count)
        low_src, high_src = pl.ds(DEEP + CZ - near - count, count), pl.ds(DEEP + near, count)
        up_copies.append(remote(part(low_src, mine_rows), part(low, mine_rows), lo_send.at[at], lo_recv.at[at], up))
        down_copies.append(
            remote(part(high_src, mine_rows), part(high, mine_rows), hi_send.at[at], hi_recv.at[at], down)
        )
        near += count

    def start(piece):
        up_copies[piece].start()
        down_copies[piece].start()

    def sent(piece):
        up_copies[piece].wait_send()
        down_copies[piece].wait_send()

    one_src, one_dst = pl.ds(71 - 55 * y, 1), pl.ds(15 + 57 * y, 1)

    def ud_part(planes, rows):
        return ud.at[pl.ds(0, 2), all_tiles, planes, rows, :]

    inner = pl.ds(1, CZ)
    ud_copies = [
        remote(ud_part(CZ, mine_rows), ud_part(0, mine_rows), ud_send.at[0], ud_recv.at[0], up),
        remote(ud_part(1, mine_rows), ud_part(CZ + 1, mine_rows), ud_send.at[1], ud_recv.at[1], down),
        remote(ud_part(inner, one_src), ud_part(inner, one_dst), ud_send.at[2], ud_recv.at[2], side),
        remote(ud_part(CZ, one_src), ud_part(0, one_dst), ud_send.at[3], ud_recv.at[3], side_up),
        remote(ud_part(1, one_src), ud_part(CZ + 1, one_dst), ud_send.at[4], ud_recv.at[4], side_down),
    ]

    def sweep_lines(plane, rows, size, keep=None):
        fields = ([], [], [])
        for j in range(TILES):
            density = ud[1, j, plane, rows, :]
            field = ud[0, j, plane, rows, :]
            value = stiff_floor + (1.0 - stiff_floor) * (density * density * density)
            if keep is not None:
                value = value * keep
                field = field * keep
            fields[0].append(value)
            fields[1].append(field)
            fields[2].append(value * field)
        for slot in range(3):
            for j, tile in enumerate(smooth_lanes(fields[slot])):
                smooth[slot, j, plane, rows, :] = tile
        return fields[0]

    def sweep_own(plane, _):
        for k in range(CY // 16):
            rows = pl.ds(pl.multiple_of(own + 16 * k, 8), 16)
            for j, tile in enumerate(sweep_lines(plane, rows, 16)):
                stiff[j, plane, rows, :] = tile
        return 0

    def volume_plane(plane, total):
        for j in range(TILES):
            here = lab_out[plane, :, 128 * j : 128 * j + 128] == 0
            value = jnp.where(here, ud[1, j, plane + 1, mine_rows, :], 0.0)
            total = total + jnp.sum(value.reshape(CY // 8, 8, 128), axis=0)
        return total

    pl.semaphore_wait(barrier, len(greeted))
    start(0)
    for copy in side_copies:
        copy.start()
    for copy in loads[3:]:
        copy.wait()
    volume = lax.fori_loop(0, CZ, volume_plane, jnp.zeros((8, 128), F32))
    lax.fori_loop(1, 4, sweep_own, 0)
    sent(0)
    start(1)
    lax.fori_loop(4, 6, sweep_own, 0)
    sent(1)
    start(2)

    def across(ref, j, plane, start, rows):
        over = ref[j, plane - 1, pl.ds(start, rows), :] + ref[j, plane + 1, pl.ds(start, rows), :]
        return over + (ref[j, plane, pl.ds(start - 1, rows), :] + ref[j, plane, pl.ds(start + 1, rows), :])

    def factor(row, j, rows):
        return jnp.broadcast_to(factors[row : row + 1, 128 * j : 128 * j + 128], (rows, 128))

    body = pl.ds(8, 72)

    def put(ref, j, plane, value, keep):
        ref[j, plane, body, :] = value if keep is None else value * keep

    def level3(plane, keep=None):
        for j in range(TILES):
            value = factor(0, j, 72) * e[j, plane, body, :] - (2.0 * NEAR * GAMMA[4]) * across(e, j, plane, 8, 72)
            put(b3, j, plane, value, keep)

    def level2(plane, keep=None):
        for j in range(TILES):
            value = (GAMMA[2] - GAMMA[4]) * e[j, plane, body, :] + factor(1, j, 72) * b3[j, plane, body, :]
            put(b2, j, plane, value - (2.0 * NEAR) * across(b3, j, plane, 8, 72), keep)

    def level1(plane, keep=None):
        for j in range(TILES):
            value = GAMMA[1] * e[j, plane, body, :] + factor(1, j, 72) * b2[j, plane, body, :]
            value = value - b3[j, plane, body, :]
            put(b1, j, plane, value - (2.0 * NEAR) * across(b2, j, plane, 8, 72), keep)

    def level0(plane, slot):
        for j in range(TILES):
            value = GAMMA[0] * e[j, plane, mine_rows, :] + factor(2, j, CY) * b1[j, plane, mine_rows, :]
            value = value - b2[j, plane, mine_rows, :]
            flat[slot, :, 128 * j : 128 * j + 128] = value - NEAR * across(b1, j, plane, own, CY)

    def repeat(level, first, last):
        def step(plane, _):
            level(plane)
            return 0

        lax.fori_loop(first, last, step, 0)

    side_copies[0].wait_recv()
    repeat(level3, 5, 11)
    repeat(level2, 6, 10)
    repeat(level1, 7, 9)
    side_copies[1].wait_recv()
    side_copies[2].wait_recv()

    sent(2)
    for copy in ud_copies:
        copy.start()
    low_keep = jnp.where(z == 0, 0.0, 1.0).astype(F32)
    high_keep = jnp.where(z == GZ - 1, 0.0, 1.0).astype(F32)

    def keep_of(plane):
        return low_keep if plane < DEEP else high_keep if plane >= DEEP + CZ else None

    def back(first, count, planes, total):
        value = transform(flat[first : first + count].reshape(count * CY, NX), basis)
        for k, plane in enumerate(planes):
            kept = jnp.where(lab_out[plane] == 0, value[CY * k : CY * k + CY], 0.0)
            filt_out[plane] = kept
            total = total + jnp.sum(jnp.abs(kept).reshape(CY // 8, 8, NX), axis=0)
        return total

    total = jnp.zeros((8, NX), F32)
    order = []
    for d in range(1, DEEP + 1):
        if d in FIRSTS:
            up_copies[FIRSTS[d]].wait_recv()
            down_copies[FIRSTS[d]].wait_recv()

        @pl.when(z == 0)
        def _():
            e[:, DEEP - d] = jnp.zeros((TILES, ROWS, 128), F32)

        @pl.when(z == GZ - 1)
        def _():
            e[:, DEEP + CZ - 1 + d] = jnp.zeros((TILES, ROWS, 128), F32)

        for level, low in ((level3, 5 - d), (level2, 6 - d), (level1, 7 - d)):
            for plane in (low, FZ - 1 - low):
                level(plane, keep_of(plane))
        for low in (8 - d, FZ - 1 - (8 - d)):
            level0(low, len(order))
            order.append(low - DEEP)
        if d == DEEP - 1:
            total = back(0, 6, order, total)
    total = back(6, 2, order[6:], total)

    def fold(value):
        return jnp.sum(value, axis=0, keepdims=True)

    row = lax.broadcasted_iota(jnp.int32, (8, 128), 0)
    size = total[:, :128] + total[:, 128:256] + total[:, 256:384] + total[:, 384:]
    mine[0] = jnp.where(row < 4, fold(size), fold(volume))

    def spread(phase):
        for d in range(GROUP - 1):
            remote(mine.at[phase], got.at[phase, d], ar_send.at[phase], ar_recv.at[phase], groups[phase][d]).start()

    def gather(phase):
        pltpu.make_async_copy(got.at[phase], got.at[phase], ar_recv.at[phase]).wait()
        return mine[phase] + jnp.sum(got[phase], axis=0)

    spread(0)

    lax.fori_loop(6, CZ + 1, sweep_own, 0)
    def sweep_out(plane, _):
        for slot in range(3):
            for j in range(TILES):
                column[slot, j, body, :] = smooth[slot, j, plane + 1, body, :] + 0.5 * (
                    smooth[slot, j, plane, body, :] + smooth[slot, j, plane + 2, body, :]
                )
        for j in range(TILES):
            lanes = slice(128 * j, 128 * j + 128)

            def stack(slot):
                return column[slot, j, mine_rows, :] + 0.5 * (
                    column[slot, j, pl.ds(own - 1, CY), :] + column[slot, j, pl.ds(own + 1, CY), :]
                )

            value = stiff[j, plane + 1, mine_rows, :]
            field = ud[0, j, plane + 1, mine_rows, :]
            diagonal = 6.0 * value + stack(0)
            offsum = value * (stack(1) - 2.0 * field) + stack(2)
            applied = diagonal * field - offsum
            updated = field + relax_omega * (load_v[plane, :, lanes] - applied) / diagonal
            adj_out[plane, :, lanes] = jnp.where(lab_out[plane, :, lanes] == 2, 0.0, updated)
        return 0

    mine[1] = gather(0)
    spread(1)

    for copy in ud_copies:
        copy.wait_recv()

    for plane, keep in ((0, low_keep), (CZ + 1, high_keep)):
        for k in range(3):
            sweep_lines(plane, pl.ds(8 + 24 * k, 24), 24, keep)

    def sweep_partner(plane, _):
        sweep_lines(plane, partner, 8)
        return 0

    lax.fori_loop(1, CZ + 1, sweep_partner, 0)

    lax.fori_loop(0, CZ, sweep_out, 0)

    tot_out[...] = gather(1)
    for phase in range(2):
        pltpu.make_async_copy(got.at[phase], got.at[phase], ar_send.at[phase]).wait()
    for copy in side_copies + ud_copies:
        copy.wait_send()


def last_kernel(filt, adj_in, labels, tot, dir_out, adj_out, held, sem):
    whole = pltpu.make_async_copy(adj_in, adj_out, sem.at[CZ])
    whole.start()
    cells = float(GZ * CZ * GY * CY * NX)
    magnitude = jnp.sum(tot[0:1, :], axis=1, keepdims=True)
    volume = jnp.sum(tot[4:5, :], axis=1, keepdims=True)
    scale = 1.0 / (magnitude / cells + epsilon)
    offset = volume_penalty * (volume / cells - volume_target)
    scale = jnp.broadcast_to(scale, (CY, NX))
    offset = jnp.broadcast_to(offset, (CY, NX))
    copies = []
    for plane in range(CZ):
        held[plane] = jnp.where(labels[plane] == 0, filt[plane] * scale - offset, 0.0)
        copy = pltpu.make_async_copy(held.at[plane], dir_out.at[plane], sem.at[plane])
        copy.start()
        copies.append(copy)
    for copy in copies + [whole]:
        copy.wait()


def on_device(sensitivity, density, load, adjoint, labels):
    shape = (CZ, CY, NX)
    dma = pltpu.SemaphoreType.DMA
    vmem = pl.BlockSpec(memory_space=pltpu.VMEM)
    hbm = pl.BlockSpec(memory_space=pltpu.HBM)
    arrays = (sensitivity, density, load, adjoint, labels, jnp.asarray(BASIS), jnp.asarray(FACTORS))
    filtered, swept, held_labels, totals = pl.pallas_call(
        main_kernel,
        out_shape=(
            pltpu.VMEM(shape, F32),
            pltpu.VMEM(shape, F32),
            pltpu.VMEM(shape, jnp.int32),
            pltpu.VMEM((8, 128), F32),
        ),
        in_specs=[hbm] * 7,
        out_specs=(vmem,) * 4,
        scratch_shapes=[
            pltpu.VMEM(shape, F32),
            pltpu.VMEM((2, NX, NX), jnp.bfloat16),
            pltpu.VMEM((8, NX), F32),
            pltpu.VMEM((TILES, FZ, ROWS, 128), F32),
            pltpu.VMEM((TILES, FZ, ROWS, 128), F32),
            pltpu.VMEM((TILES, FZ, ROWS, 128), F32),
            pltpu.VMEM((TILES, FZ, ROWS, 128), F32),
            pltpu.VMEM(shape, F32),
            pltpu.VMEM((2, TILES, CZ + 2, ROWS, 128), F32),
            pltpu.VMEM((TILES, CZ + 2, ROWS, 128), F32),
            pltpu.VMEM((3, TILES, CZ + 2, ROWS, 128), F32),
            pltpu.VMEM((3, TILES, ROWS, 128), F32),
            pltpu.VMEM(shape, F32),
            pltpu.VMEM((2, 8, 128), F32),
            pltpu.VMEM((2, GROUP - 1, 8, 128), F32),
            dma((5 + 2 * TILES,)),
            dma((len(PIECES),)),
            dma((len(PIECES),)),
            dma((len(PIECES),)),
            dma((len(PIECES),)),
            dma((3,)),
            dma((3,)),
            dma((5,)),
            dma((5,)),
            dma((2,)),
            dma((2,)),
        ],
        compiler_params=pltpu.CompilerParams(
            collective_id=1, has_side_effects=True, vmem_limit_bytes=40 * 2**20
        ),
        name="filter_and_sweep",
    )(*[pltpu.with_memory_space_constraint(array, pltpu.HBM) for array in arrays])
    filtered, swept, held_labels, totals = (
        pltpu.with_memory_space_constraint(array, pltpu.VMEM) for array in (filtered, swept, held_labels, totals)
    )
    return pl.pallas_call(
        last_kernel,
        out_shape=(jax.ShapeDtypeStruct(shape, F32), jax.ShapeDtypeStruct(shape, F32)),
        in_specs=[vmem] * 4,
        out_specs=(hbm, hbm),
        scratch_shapes=[pltpu.VMEM(shape, F32), dma((CZ + 1,))],
        name="normalise_and_store",
    )(filtered, swept, held_labels, totals)


def solution(mesh):
    placed = (P("gz", "gy", None),) * 5
    return jax.shard_map(
        on_device,
        mesh=mesh,
        in_specs=placed,
        out_specs=(P("gz", "gy", None), P("gz", "gy", None)),
        check_vma=False,
    )
```

```python
import functools

import numpy as np
import jax
import jax.numpy as jnp
from jax import lax
from jax.experimental import pallas as pl
from jax.experimental.pallas import tpu as pltpu
from jax.sharding import PartitionSpec as P

ITERS = 4
filter_weight = 8.0
stiff_floor = 0.05
relax_omega = 0.6
volume_target = 0.15
volume_penalty = 20.0
epsilon = 1e-06
center_diag = 1.0 + 6.0 * filter_weight
lower_eig = 1.0 / center_diag
upper_eig = (1.0 + 12.0 * filter_weight) / center_diag
middle_eig = (upper_eig + lower_eig) / 2.0
half_width = (upper_eig - lower_eig) / 2.0
sigma_ratio = middle_eig / half_width

MESH = pl.DeviceIdType.MESH
F32 = jnp.float32

CZ, CY, NX = 8, 64, 512
GZ, GY = 128, 2
GROUP = 16
ROWS = CY + 24
DEEP = ITERS
FZ = CZ + 2 * DEEP
PIECES = (2, 1, 1)
FIRSTS = {1: 0, 3: 1, 4: 2}


def filter_coefficients():
    times_t = np.polynomial.chebyshev.chebmulx
    residue = np.zeros(ITERS + 2)
    residue[0] = 1.0

    def pad(series):
        return np.pad(series, (0, max(0, ITERS + 2 - len(series))))[: ITERS + 2]

    def apply(series):
        return center_diag * (middle_eig * series + half_width * pad(times_t(series)))

    update = residue / (center_diag * middle_eig)
    result = update.copy()
    ratio_prev = 1.0 / sigma_ratio
    for _ in range(ITERS):
        residue = residue - apply(update)
        ratio_next = 1.0 / (2.0 * sigma_ratio - ratio_prev)
        update = ratio_next * ratio_prev * update + 2.0 * ratio_next / half_width * (
            residue / center_diag
        )
        ratio_prev = ratio_next
        result = result + update
    return [float(value) for value in result[: ITERS + 1]]


GAMMA = filter_coefficients()
SELF = (1.0 - middle_eig) / half_width
NEAR = filter_weight / (center_diag * half_width)
TILES = NX // 128


def hops(*offsets):
    return sum(min(offset, size - offset) for offset, size in offsets)


LINE = sorted(
    [(dz, dc) for dz in range(8) for dc in range(2) if dz or dc],
    key=lambda at: (-hops((at[0], 8)), at),
)
PLANE = sorted(
    [(dy, dx) for dy in range(4) for dx in range(4) if dy or dx],
    key=lambda at: (-hops((at[0], 4), (at[1], 4)), at),
)


def sine_basis():
    index = np.arange(1, NX + 1, dtype=np.float64)
    basis = np.sqrt(2.0 / (NX + 1)) * np.sin(np.pi * np.outer(index, index) / (NX + 1))
    high = basis.astype(jnp.bfloat16)
    low = (basis - high.astype(np.float64)).astype(jnp.bfloat16)
    along = 2.0 * np.cos(np.pi * index / (NX + 1))
    factors = np.zeros((8, NX))
    factors[0] = GAMMA[3] + 2.0 * GAMMA[4] * (SELF - NEAR * along)
    factors[1] = 2.0 * (SELF - NEAR * along)
    factors[2] = SELF - NEAR * along
    return np.stack([high, low]), factors.astype(np.float32)


BASIS, FACTORS = sine_basis()


def transform(value, basis):
    high = value.astype(jnp.bfloat16)
    low = (value - high.astype(F32)).astype(jnp.bfloat16)
    first = jnp.dot(high, basis[0], preferred_element_type=F32)
    second = jnp.dot(low, basis[0], preferred_element_type=F32)
    third = jnp.dot(high, basis[1], preferred_element_type=F32)
    return first + (second + third)


def smooth_lanes(tiles):
    lane = lax.broadcasted_iota(jnp.int32, tiles[0].shape, 1)
    from_left = [pltpu.roll(tile, 1, 1) for tile in tiles]
    from_right = [pltpu.roll(tile, 127, 1) for tile in tiles]
    out = []
    for j, tile in enumerate(tiles):
        left = jnp.where(lane == 0, from_left[j - 1] if j > 0 else 0.0, from_left[j])
        right = jnp.where(lane == 127, from_right[j + 1] if j + 1 < TILES else 0.0, from_right[j])
        out.append(tile + 0.5 * (left + right))
    return out


def main_kernel(
    sens, dens, load, adj, labels, basis_in, factors_in,
    filt_out, adj_out, lab_out, tot_out,
    raw, basis, factors, e, b3, b2, b1, flat, ud, stiff, smooth, column, load_v, mine, got,
    in_sem, lo_send, lo_recv, hi_send, hi_recv, side_send, side_recv, ud_send, ud_recv, ar_send, ar_recv, met,
):
    z = lax.axis_index("gz")
    y = lax.axis_index("gy")
    up = (lax.rem(z + 1, GZ), y)
    down = (lax.rem(z + GZ - 1, GZ), y)
    side = (z, 1 - y)
    side_up = (up[0], 1 - y)
    side_down = (down[0], 1 - y)
    block = z // GROUP
    rank = lax.rem(z, GROUP)
    chip, core = rank // 2, lax.rem(rank, 2)
    across_y, across_x = block // 2, 2 * y + lax.rem(block, 2)
    groups = ([], [])
    for dz, dc in LINE:
        groups[0].append((block * GROUP + 2 * lax.rem(chip + dz, 8) + lax.rem(core + dc, 2), y))
    for dy, dx in PLANE:
        other_y, other_x = lax.rem(across_y + dy, 4), lax.rem(across_x + dx, 4)
        groups[1].append(((2 * other_y + lax.rem(other_x, 2)) * GROUP + rank, other_x // 2))

    near = [(block * GROUP + lax.rem(rank + d, GROUP), y) for d in (1, 2, 14, 15)]
    at_y, at_x = block // 2, 2 * y + lax.rem(block, 2)
    for dy, dx in ((0, 1), (0, 3), (1, 0), (3, 0)):
        to_y, to_x = lax.rem(at_y + dy, 4), lax.rem(at_x + dx, 4)
        near.append(((2 * to_y + lax.rem(to_x, 2)) * GROUP + rank, to_x // 2))
    told = near + [side]

    def tell(turn):
        for device in told:
            pl.semaphore_signal(met.at[turn], inc=1, device_id=device, device_id_type=MESH)

    def heard(turn):
        pl.semaphore_wait(met.at[turn], len(told))

    own = pl.multiple_of(8 + 8 * y, 8)
    mine_rows = pl.ds(own, CY)
    partner = pl.ds(pl.multiple_of(72 - 64 * y, 8), 8)
    all_tiles = pl.ds(0, TILES)
    loads = [
        pltpu.make_async_copy(sens, raw, in_sem.at[0]),
        pltpu.make_async_copy(basis_in, basis, in_sem.at[1]),
        pltpu.make_async_copy(factors_in, factors, in_sem.at[2]),
        pltpu.make_async_copy(labels, lab_out, in_sem.at[3]),
        pltpu.make_async_copy(load, load_v, in_sem.at[4]),
    ]
    for j in range(TILES):
        for slot, array in enumerate((adj, dens)):
            loads.append(
                pltpu.make_async_copy(
                    array.at[:, :, pl.ds(128 * j, 128)],
                    ud.at[slot, j, pl.ds(1, CZ), mine_rows, :],
                    in_sem.at[5 + 2 * j + slot],
                )
            )
    for copy in loads[:3]:
        copy.start()

    e[:, :, partner, :] = jnp.zeros((TILES, FZ, 8, 128), F32)
    ud[:, :, :, partner, :] = jnp.zeros((2, TILES, CZ + 2, 8, 128), F32)

    barrier = pltpu.get_barrier_semaphore()
    greeted = [up, down, side, side_up, side_down] + near
    for device in greeted:
        pl.semaphore_signal(barrier, inc=1, device_id=device, device_id_type=MESH)
    for copy in loads[3:]:
        copy.start()

    def clear(j, _):
        for ref in (e, b3, b2, b1):
            ref[j, :, 0:8, :] = jnp.zeros((FZ, 8, 128), F32)
            ref[j, :, 80:88, :] = jnp.zeros((FZ, 8, 128), F32)
        for slot in range(3):
            smooth[slot, j, :, 0:8, :] = jnp.zeros((CZ + 2, 8, 128), F32)
            smooth[slot, j, :, 80:88, :] = jnp.zeros((CZ + 2, 8, 128), F32)
            column[slot, j, 0:8, :] = jnp.zeros((8, 128), F32)
            column[slot, j, 80:88, :] = jnp.zeros((8, 128), F32)
        return 0

    loads[0].wait()
    loads[1].wait()
    loads[2].wait()
    spectrum = transform(raw[...].reshape(CZ * CY, NX), basis)
    for plane in range(CZ):
        for j in range(TILES):
            e[j, DEEP + plane, mine_rows, :] = spectrum[CY * plane : CY * plane + CY, 128 * j : 128 * j + 128]

    four_src, four_dst = pl.ds(68 - 52 * y, 4), pl.ds(12 + 60 * y, 4)
    three_src, three_dst = pl.ds(69 - 53 * y, 3), pl.ds(13 + 59 * y, 3)

    def remote(src, dst, send, recv, device):
        return pltpu.make_async_remote_copy(src, dst, send, recv, device_id=device, device_id_type=MESH)

    def part(planes, rows):
        return e.at[all_tiles, planes, rows, :]

    side_copies = [
        remote(part(pl.ds(4, 8), four_src), part(pl.ds(4, 8), four_dst), side_send.at[0], side_recv.at[0], side),
        remote(part(pl.ds(9, 3), three_src), part(pl.ds(1, 3), three_dst), side_send.at[1], side_recv.at[1], side_up),
        remote(part(pl.ds(4, 3), three_src), part(pl.ds(12, 3), three_dst), side_send.at[2], side_recv.at[2], side_down),
    ]
    up_copies, down_copies = [], []
    near = 0
    for at, count in enumerate(PIECES):
        low, high = pl.ds(DEEP - near - count, count), pl.ds(DEEP + CZ + near, count)
        low_src, high_src = pl.ds(DEEP + CZ - near - count, count), pl.ds(DEEP + near, count)
        up_copies.append(remote(part(low_src, mine_rows), part(low, mine_rows), lo_send.at[at], lo_recv.at[at], up))
        down_copies.append(
            remote(part(high_src, mine_rows), part(high, mine_rows), hi_send.at[at], hi_recv.at[at], down)
        )
        near += count

    def start(piece):
        up_copies[piece].start()
        down_copies[piece].start()

    def sent(piece):
        up_copies[piece].wait_send()
        down_copies[piece].wait_send()

    one_src, one_dst = pl.ds(71 - 55 * y, 1), pl.ds(15 + 57 * y, 1)

    def ud_part(planes, rows):
        return ud.at[pl.ds(0, 2), all_tiles, planes, rows, :]

    inner = pl.ds(1, CZ)
    ud_copies = [
        remote(ud_part(CZ, mine_rows), ud_part(0, mine_rows), ud_send.at[0], ud_recv.at[0], up),
        remote(ud_part(1, mine_rows), ud_part(CZ + 1, mine_rows), ud_send.at[1], ud_recv.at[1], down),
        remote(ud_part(inner, one_src), ud_part(inner, one_dst), ud_send.at[2], ud_recv.at[2], side),
        remote(ud_part(CZ, one_src), ud_part(0, one_dst), ud_send.at[3], ud_recv.at[3], side_up),
        remote(ud_part(1, one_src), ud_part(CZ + 1, one_dst), ud_send.at[4], ud_recv.at[4], side_down),
    ]

    def sweep_lines(plane, rows, size, keep=None):
        fields = ([], [], [])
        for j in range(TILES):
            density = ud[1, j, plane, rows, :]
            field = ud[0, j, plane, rows, :]
            value = stiff_floor + (1.0 - stiff_floor) * (density * density * density)
            if keep is not None:
                value = value * keep
                field = field * keep
            fields[0].append(value)
            fields[1].append(field)
            fields[2].append(value * field)
        for slot in range(3):
            for j, tile in enumerate(smooth_lanes(fields[slot])):
                smooth[slot, j, plane, rows, :] = tile
        return fields[0]

    def sweep_own(plane, _):
        for k in range(CY // 16):
            rows = pl.ds(pl.multiple_of(own + 16 * k, 8), 16)
            for j, tile in enumerate(sweep_lines(plane, rows, 16)):
                stiff[j, plane, rows, :] = tile
        return 0

    def volume_plane(plane, total):
        for j in range(TILES):
            here = lab_out[plane, :, 128 * j : 128 * j + 128] == 0
            value = jnp.where(here, ud[1, j, plane + 1, mine_rows, :], 0.0)
            total = total + jnp.sum(value.reshape(CY // 8, 8, 128), axis=0)
        return total

    pl.semaphore_wait(barrier, len(greeted))
    start(0)
    for copy in side_copies:
        copy.start()
    tell(0)
    lax.fori_loop(0, TILES, clear, 0)
    for copy in loads[3:]:
        copy.wait()
    volume = lax.fori_loop(0, CZ, volume_plane, jnp.zeros((8, 128), F32))
    lax.fori_loop(1, 4, sweep_own, 0)
    sent(0)
    start(1)
    lax.fori_loop(4, 6, sweep_own, 0)
    sent(1)
    start(2)
    heard(0)
    tell(1)

    def across(ref, j, plane, start, rows):
        over = ref[j, plane - 1, pl.ds(start, rows), :] + ref[j, plane + 1, pl.ds(start, rows), :]
        return over + (ref[j, plane, pl.ds(start - 1, rows), :] + ref[j, plane, pl.ds(start + 1, rows), :])

    def factor(row, j, rows):
        return jnp.broadcast_to(factors[row : row + 1, 128 * j : 128 * j + 128], (rows, 128))

    body = pl.ds(8, 72)

    def put(ref, j, plane, value, keep):
        ref[j, plane, body, :] = value if keep is None else value * keep

    def level3(plane, keep=None):
        for j in range(TILES):
            value = factor(0, j, 72) * e[j, plane, body, :] - (2.0 * NEAR * GAMMA[4]) * across(e, j, plane, 8, 72)
            put(b3, j, plane, value, keep)

    def level2(plane, keep=None):
        for j in range(TILES):
            value = (GAMMA[2] - GAMMA[4]) * e[j, plane, body, :] + factor(1, j, 72) * b3[j, plane, body, :]
            put(b2, j, plane, value - (2.0 * NEAR) * across(b3, j, plane, 8, 72), keep)

    def level1(plane, keep=None):
        for j in range(TILES):
            value = GAMMA[1] * e[j, plane, body, :] + factor(1, j, 72) * b2[j, plane, body, :]
            value = value - b3[j, plane, body, :]
            put(b1, j, plane, value - (2.0 * NEAR) * across(b2, j, plane, 8, 72), keep)

    def level0(plane, slot):
        for j in range(TILES):
            value = GAMMA[0] * e[j, plane, mine_rows, :] + factor(2, j, CY) * b1[j, plane, mine_rows, :]
            value = value - b2[j, plane, mine_rows, :]
            flat[slot, :, 128 * j : 128 * j + 128] = value - NEAR * across(b1, j, plane, own, CY)

    def repeat(level, first, last):
        def step(plane, _):
            level(plane)
            return 0

        lax.fori_loop(first, last, step, 0)

    side_copies[0].wait_recv()
    repeat(level3, 5, 11)
    repeat(level2, 6, 10)
    repeat(level1, 7, 9)
    side_copies[1].wait_recv()
    side_copies[2].wait_recv()
    heard(1)
    tell(2)

    sent(2)
    for copy in ud_copies:
        copy.start()
    low_keep = jnp.where(z == 0, 0.0, 1.0).astype(F32)
    high_keep = jnp.where(z == GZ - 1, 0.0, 1.0).astype(F32)

    def keep_of(plane):
        return low_keep if plane < DEEP else high_keep if plane >= DEEP + CZ else None

    def back(first, count, planes, total):
        value = transform(flat[first : first + count].reshape(count * CY, NX), basis)
        for k, plane in enumerate(planes):
            kept = jnp.where(lab_out[plane] == 0, value[CY * k : CY * k + CY], 0.0)
            filt_out[plane] = kept
            total = total + jnp.sum(jnp.abs(kept).reshape(CY // 8, 8, NX), axis=0)
        return total

    total = jnp.zeros((8, NX), F32)
    order = []
    for d in range(1, DEEP + 1):
        if d in FIRSTS:
            up_copies[FIRSTS[d]].wait_recv()
            down_copies[FIRSTS[d]].wait_recv()

        @pl.when(z == 0)
        def _():
            e[:, DEEP - d] = jnp.zeros((TILES, ROWS, 128), F32)

        @pl.when(z == GZ - 1)
        def _():
            e[:, DEEP + CZ - 1 + d] = jnp.zeros((TILES, ROWS, 128), F32)

        for level, low in ((level3, 5 - d), (level2, 6 - d), (level1, 7 - d)):
            for plane in (low, FZ - 1 - low):
                level(plane, keep_of(plane))
        for low in (8 - d, FZ - 1 - (8 - d)):
            level0(low, len(order))
            order.append(low - DEEP)
        if d == DEEP - 1:
            total = back(0, 6, order, total)
    total = back(6, 2, order[6:], total)

    def fold(value):
        return jnp.sum(value, axis=0, keepdims=True)

    row = lax.broadcasted_iota(jnp.int32, (8, 128), 0)
    size = total[:, :128] + total[:, 128:256] + total[:, 256:384] + total[:, 384:]
    mine[0] = jnp.where(row < 4, fold(size), fold(volume))

    def spread(phase):
        for d in range(GROUP - 1):
            remote(mine.at[phase], got.at[phase, d], ar_send.at[phase], ar_recv.at[phase], groups[phase][d]).start()

    def gather(phase):
        pltpu.make_async_copy(got.at[phase], got.at[phase], ar_recv.at[phase]).wait()
        return mine[phase] + jnp.sum(got[phase], axis=0)

    heard(2)
    spread(0)

    lax.fori_loop(6, CZ + 1, sweep_own, 0)
    def sweep_out(plane, _):
        for slot in range(3):
            for j in range(TILES):
                column[slot, j, body, :] = smooth[slot, j, plane + 1, body, :] + 0.5 * (
                    smooth[slot, j, plane, body, :] + smooth[slot, j, plane + 2, body, :]
                )
        for j in range(TILES):
            lanes = slice(128 * j, 128 * j + 128)

            def stack(slot):
                return column[slot, j, mine_rows, :] + 0.5 * (
                    column[slot, j, pl.ds(own - 1, CY), :] + column[slot, j, pl.ds(own + 1, CY), :]
                )

            value = stiff[j, plane + 1, mine_rows, :]
            field = ud[0, j, plane + 1, mine_rows, :]
            diagonal = 6.0 * value + stack(0)
            offsum = value * (stack(1) - 2.0 * field) + stack(2)
            applied = diagonal * field - offsum
            updated = field + relax_omega * (load_v[plane, :, lanes] - applied) / diagonal
            adj_out[plane, :, lanes] = jnp.where(lab_out[plane, :, lanes] == 2, 0.0, updated)
        return 0

    mine[1] = gather(0)
    spread(1)

    for copy in ud_copies:
        copy.wait_recv()

    for plane, keep in ((0, low_keep), (CZ + 1, high_keep)):
        for k in range(3):
            sweep_lines(plane, pl.ds(8 + 24 * k, 24), 24, keep)

    def sweep_partner(plane, _):
        sweep_lines(plane, partner, 8)
        return 0

    lax.fori_loop(1, CZ + 1, sweep_partner, 0)

    lax.fori_loop(0, CZ, sweep_out, 0)

    tot_out[...] = gather(1)
    for phase in range(2):
        pltpu.make_async_copy(got.at[phase], got.at[phase], ar_send.at[phase]).wait()
    for copy in side_copies + ud_copies:
        copy.wait_send()


def last_kernel(filt, adj_in, labels, tot, dir_out, adj_out, held, sem):
    whole = pltpu.make_async_copy(adj_in, adj_out, sem.at[CZ])
    whole.start()
    cells = float(GZ * CZ * GY * CY * NX)
    magnitude = jnp.sum(tot[0:1, :], axis=1, keepdims=True)
    volume = jnp.sum(tot[4:5, :], axis=1, keepdims=True)
    scale = 1.0 / (magnitude / cells + epsilon)
    offset = volume_penalty * (volume / cells - volume_target)
    scale = jnp.broadcast_to(scale, (CY, NX))
    offset = jnp.broadcast_to(offset, (CY, NX))
    copies = []
    for plane in range(CZ):
        held[plane] = jnp.where(labels[plane] == 0, filt[plane] * scale - offset, 0.0)
        copy = pltpu.make_async_copy(held.at[plane], dir_out.at[plane], sem.at[plane])
        copy.start()
        copies.append(copy)
    for copy in copies + [whole]:
        copy.wait()


def on_device(sensitivity, density, load, adjoint, labels):
    shape = (CZ, CY, NX)
    dma = pltpu.SemaphoreType.DMA
    vmem = pl.BlockSpec(memory_space=pltpu.VMEM)
    hbm = pl.BlockSpec(memory_space=pltpu.HBM)
    arrays = (sensitivity, density, load, adjoint, labels, jnp.asarray(BASIS), jnp.asarray(FACTORS))
    filtered, swept, held_labels, totals = pl.pallas_call(
        main_kernel,
        out_shape=(
            pltpu.VMEM(shape, F32),
            pltpu.VMEM(shape, F32),
            pltpu.VMEM(shape, jnp.int32),
            pltpu.VMEM((8, 128), F32),
        ),
        in_specs=[hbm] * 7,
        out_specs=(vmem,) * 4,
        scratch_shapes=[
            pltpu.VMEM(shape, F32),
            pltpu.VMEM((2, NX, NX), jnp.bfloat16),
            pltpu.VMEM((8, NX), F32),
            pltpu.VMEM((TILES, FZ, ROWS, 128), F32),
            pltpu.VMEM((TILES, FZ, ROWS, 128), F32),
            pltpu.VMEM((TILES, FZ, ROWS, 128), F32),
            pltpu.VMEM((TILES, FZ, ROWS, 128), F32),
            pltpu.VMEM(shape, F32),
            pltpu.VMEM((2, TILES, CZ + 2, ROWS, 128), F32),
            pltpu.VMEM((TILES, CZ + 2, ROWS, 128), F32),
            pltpu.VMEM((3, TILES, CZ + 2, ROWS, 128), F32),
            pltpu.VMEM((3, TILES, ROWS, 128), F32),
            pltpu.VMEM(shape, F32),
            pltpu.VMEM((2, 8, 128), F32),
            pltpu.VMEM((2, GROUP - 1, 8, 128), F32),
            dma((5 + 2 * TILES,)),
            dma((len(PIECES),)),
            dma((len(PIECES),)),
            dma((len(PIECES),)),
            dma((len(PIECES),)),
            dma((3,)),
            dma((3,)),
            dma((5,)),
            dma((5,)),
            dma((2,)),
            dma((2,)),
            pltpu.SemaphoreType.REGULAR((3,)),
        ],
        compiler_params=pltpu.CompilerParams(
            collective_id=1, has_side_effects=True, vmem_limit_bytes=40 * 2**20
        ),
        name="filter_and_sweep",
    )(*[pltpu.with_memory_space_constraint(array, pltpu.HBM) for array in arrays])
    filtered, swept, held_labels, totals = (
        pltpu.with_memory_space_constraint(array, pltpu.VMEM) for array in (filtered, swept, held_labels, totals)
    )
    return pl.pallas_call(
        last_kernel,
        out_shape=(jax.ShapeDtypeStruct(shape, F32), jax.ShapeDtypeStruct(shape, F32)),
        in_specs=[vmem] * 4,
        out_specs=(hbm, hbm),
        scratch_shapes=[pltpu.VMEM(shape, F32), dma((CZ + 1,))],
        name="normalise_and_store",
    )(filtered, swept, held_labels, totals)


def solution(mesh):
    placed = (P("gz", "gy", None),) * 5
    return jax.shard_map(
        on_device,
        mesh=mesh,
        in_specs=placed,
        out_specs=(P("gz", "gy", None), P("gz", "gy", None)),
        check_vma=False,
    )
```

```python
import functools

import numpy as np
import jax
import jax.numpy as jnp
from jax import lax
from jax.experimental import pallas as pl
from jax.experimental.pallas import tpu as pltpu
from jax.sharding import PartitionSpec as P

ITERS = 4
filter_weight = 8.0
stiff_floor = 0.05
relax_omega = 0.6
volume_target = 0.15
volume_penalty = 20.0
epsilon = 1e-06
center_diag = 1.0 + 6.0 * filter_weight
lower_eig = 1.0 / center_diag
upper_eig = (1.0 + 12.0 * filter_weight) / center_diag
middle_eig = (upper_eig + lower_eig) / 2.0
half_width = (upper_eig - lower_eig) / 2.0
sigma_ratio = middle_eig / half_width

MESH = pl.DeviceIdType.MESH
F32 = jnp.float32

CZ, CY, NX = 8, 64, 512
GZ, GY = 128, 2
GROUP = 16
ROWS = CY + 24
DEEP = ITERS
FZ = CZ + 2 * DEEP
PIECES = (2, 2)
FIRSTS = {1: 0, 3: 1}


def filter_coefficients():
    times_t = np.polynomial.chebyshev.chebmulx
    residue = np.zeros(ITERS + 2)
    residue[0] = 1.0

    def pad(series):
        return np.pad(series, (0, max(0, ITERS + 2 - len(series))))[: ITERS + 2]

    def apply(series):
        return center_diag * (middle_eig * series + half_width * pad(times_t(series)))

    update = residue / (center_diag * middle_eig)
    result = update.copy()
    ratio_prev = 1.0 / sigma_ratio
    for _ in range(ITERS):
        residue = residue - apply(update)
        ratio_next = 1.0 / (2.0 * sigma_ratio - ratio_prev)
        update = ratio_next * ratio_prev * update + 2.0 * ratio_next / half_width * (
            residue / center_diag
        )
        ratio_prev = ratio_next
        result = result + update
    return [float(value) for value in result[: ITERS + 1]]


GAMMA = filter_coefficients()
SELF = (1.0 - middle_eig) / half_width
NEAR = filter_weight / (center_diag * half_width)
TILES = NX // 128


def hops(*offsets):
    return sum(min(offset, size - offset) for offset, size in offsets)


LINE = sorted(
    [(dz, dc) for dz in range(8) for dc in range(2) if dz or dc],
    key=lambda at: (-hops((at[0], 8)), at),
)
PLANE = sorted(
    [(dy, dx) for dy in range(4) for dx in range(4) if dy or dx],
    key=lambda at: (-hops((at[0], 4), (at[1], 4)), at),
)


def sine_basis():
    index = np.arange(1, NX + 1, dtype=np.float64)
    basis = np.sqrt(2.0 / (NX + 1)) * np.sin(np.pi * np.outer(index, index) / (NX + 1))
    high = basis.astype(jnp.bfloat16)
    low = (basis - high.astype(np.float64)).astype(jnp.bfloat16)
    along = 2.0 * np.cos(np.pi * index / (NX + 1))
    factors = np.zeros((8, NX))
    factors[0] = GAMMA[3] + 2.0 * GAMMA[4] * (SELF - NEAR * along)
    factors[1] = 2.0 * (SELF - NEAR * along)
    factors[2] = SELF - NEAR * along
    return np.stack([high, low]), factors.astype(np.float32)


BASIS, FACTORS = sine_basis()


def transform(value, basis):
    high = value.astype(jnp.bfloat16)
    low = (value - high.astype(F32)).astype(jnp.bfloat16)
    first = jnp.dot(high, basis[0], preferred_element_type=F32)
    second = jnp.dot(low, basis[0], preferred_element_type=F32)
    third = jnp.dot(high, basis[1], preferred_element_type=F32)
    return first + (second + third)


def smooth_lanes(tiles):
    lane = lax.broadcasted_iota(jnp.int32, tiles[0].shape, 1)
    from_left = [pltpu.roll(tile, 1, 1) for tile in tiles]
    from_right = [pltpu.roll(tile, 127, 1) for tile in tiles]
    out = []
    for j, tile in enumerate(tiles):
        left = jnp.where(lane == 0, from_left[j - 1] if j > 0 else 0.0, from_left[j])
        right = jnp.where(lane == 127, from_right[j + 1] if j + 1 < TILES else 0.0, from_right[j])
        out.append(tile + 0.5 * (left + right))
    return out


def main_kernel(
    sens, dens, load, adj, labels, basis_in, factors_in,
    filt_out, adj_out, lab_out, tot_out,
    raw, basis, factors, e, b3, b2, b1, flat, ud, stiff, smooth, column, load_v, mine, got,
    in_sem, lo_send, lo_recv, hi_send, hi_recv, side_send, side_recv, ud_send, ud_recv, ar_send, ar_recv, met,
):
    z = lax.axis_index("gz")
    y = lax.axis_index("gy")
    up = (lax.rem(z + 1, GZ), y)
    down = (lax.rem(z + GZ - 1, GZ), y)
    side = (z, 1 - y)
    side_up = (up[0], 1 - y)
    side_down = (down[0], 1 - y)
    block = z // GROUP
    rank = lax.rem(z, GROUP)
    chip, core = rank // 2, lax.rem(rank, 2)
    across_y, across_x = block // 2, 2 * y + lax.rem(block, 2)
    groups = ([], [])
    for dz, dc in LINE:
        groups[0].append((block * GROUP + 2 * lax.rem(chip + dz, 8) + lax.rem(core + dc, 2), y))
    for dy, dx in PLANE:
        other_y, other_x = lax.rem(across_y + dy, 4), lax.rem(across_x + dx, 4)
        groups[1].append(((2 * other_y + lax.rem(other_x, 2)) * GROUP + rank, other_x // 2))

    near = [(block * GROUP + lax.rem(rank + d, GROUP), y) for d in (1, 2, 14, 15)]
    at_y, at_x = block // 2, 2 * y + lax.rem(block, 2)
    for dy, dx in ((0, 1), (0, 3), (1, 0), (3, 0)):
        to_y, to_x = lax.rem(at_y + dy, 4), lax.rem(at_x + dx, 4)
        near.append(((2 * to_y + lax.rem(to_x, 2)) * GROUP + rank, to_x // 2))
    told = near + [side]

    def tell(turn):
        for device in told:
            pl.semaphore_signal(met.at[turn], inc=1, device_id=device, device_id_type=MESH)

    def heard(turn):
        pl.semaphore_wait(met.at[turn], len(told))

    own = pl.multiple_of(8 + 8 * y, 8)
    mine_rows = pl.ds(own, CY)
    partner = pl.ds(pl.multiple_of(72 - 64 * y, 8), 8)
    all_tiles = pl.ds(0, TILES)
    loads = [
        pltpu.make_async_copy(sens, raw, in_sem.at[0]),
        pltpu.make_async_copy(basis_in, basis, in_sem.at[1]),
        pltpu.make_async_copy(factors_in, factors, in_sem.at[2]),
        pltpu.make_async_copy(labels, lab_out, in_sem.at[3]),
        pltpu.make_async_copy(load, load_v, in_sem.at[4]),
    ]
    for j in range(TILES):
        for slot, array in enumerate((adj, dens)):
            loads.append(
                pltpu.make_async_copy(
                    array.at[:, :, pl.ds(128 * j, 128)],
                    ud.at[slot, j, pl.ds(1, CZ), mine_rows, :],
                    in_sem.at[5 + 2 * j + slot],
                )
            )
    for copy in loads[:3]:
        copy.start()

    e[:, :, partner, :] = jnp.zeros((TILES, FZ, 8, 128), F32)
    ud[:, :, :, partner, :] = jnp.zeros((2, TILES, CZ + 2, 8, 128), F32)

    barrier = pltpu.get_barrier_semaphore()
    greeted = [up, down, side, side_up, side_down] + near
    for device in greeted:
        pl.semaphore_signal(barrier, inc=1, device_id=device, device_id_type=MESH)
    for copy in loads[3:]:
        copy.start()

    def clear(j, _):
        for ref in (e, b3, b2, b1):
            ref[j, :, 0:8, :] = jnp.zeros((FZ, 8, 128), F32)
            ref[j, :, 80:88, :] = jnp.zeros((FZ, 8, 128), F32)
        for slot in range(3):
            smooth[slot, j, :, 0:8, :] = jnp.zeros((CZ + 2, 8, 128), F32)
            smooth[slot, j, :, 80:88, :] = jnp.zeros((CZ + 2, 8, 128), F32)
            column[slot, j, 0:8, :] = jnp.zeros((8, 128), F32)
            column[slot, j, 80:88, :] = jnp.zeros((8, 128), F32)
        return 0

    loads[0].wait()
    loads[1].wait()
    loads[2].wait()
    spectrum = transform(raw[...].reshape(CZ * CY, NX), basis)
    for plane in range(CZ):
        for j in range(TILES):
            e[j, DEEP + plane, mine_rows, :] = spectrum[CY * plane : CY * plane + CY, 128 * j : 128 * j + 128]

    four_src, four_dst = pl.ds(68 - 52 * y, 4), pl.ds(12 + 60 * y, 4)
    three_src, three_dst = pl.ds(69 - 53 * y, 3), pl.ds(13 + 59 * y, 3)

    def remote(src, dst, send, recv, device):
        return pltpu.make_async_remote_copy(src, dst, send, recv, device_id=device, device_id_type=MESH)

    def part(planes, rows):
        return e.at[all_tiles, planes, rows, :]

    side_copies = [
        remote(part(pl.ds(4, 8), four_src), part(pl.ds(4, 8), four_dst), side_send.at[0], side_recv.at[0], side),
        remote(part(pl.ds(9, 3), three_src), part(pl.ds(1, 3), three_dst), side_send.at[1], side_recv.at[1], side_up),
        remote(part(pl.ds(4, 3), three_src), part(pl.ds(12, 3), three_dst), side_send.at[2], side_recv.at[2], side_down),
    ]
    up_copies, down_copies = [], []
    near = 0
    for at, count in enumerate(PIECES):
        low, high = pl.ds(DEEP - near - count, count), pl.ds(DEEP + CZ + near, count)
        low_src, high_src = pl.ds(DEEP + CZ - near - count, count), pl.ds(DEEP + near, count)
        up_copies.append(remote(part(low_src, mine_rows), part(low, mine_rows), lo_send.at[at], lo_recv.at[at], up))
        down_copies.append(
            remote(part(high_src, mine_rows), part(high, mine_rows), hi_send.at[at], hi_recv.at[at], down)
        )
        near += count

    def start(piece):
        up_copies[piece].start()
        down_copies[piece].start()

    def sent(piece):
        up_copies[piece].wait_send()
        down_copies[piece].wait_send()

    one_src, one_dst = pl.ds(71 - 55 * y, 1), pl.ds(15 + 57 * y, 1)

    def ud_part(planes, rows):
        return ud.at[pl.ds(0, 2), all_tiles, planes, rows, :]

    inner = pl.ds(1, CZ)
    ud_copies = [
        remote(ud_part(CZ, mine_rows), ud_part(0, mine_rows), ud_send.at[0], ud_recv.at[0], up),
        remote(ud_part(1, mine_rows), ud_part(CZ + 1, mine_rows), ud_send.at[1], ud_recv.at[1], down),
        remote(ud_part(inner, one_src), ud_part(inner, one_dst), ud_send.at[2], ud_recv.at[2], side),
        remote(ud_part(CZ, one_src), ud_part(0, one_dst), ud_send.at[3], ud_recv.at[3], side_up),
        remote(ud_part(1, one_src), ud_part(CZ + 1, one_dst), ud_send.at[4], ud_recv.at[4], side_down),
    ]

    def sweep_lines(plane, rows, size, keep=None):
        fields = ([], [], [])
        for j in range(TILES):
            density = ud[1, j, plane, rows, :]
            field = ud[0, j, plane, rows, :]
            value = stiff_floor + (1.0 - stiff_floor) * (density * density * density)
            if keep is not None:
                value = value * keep
                field = field * keep
            fields[0].append(value)
            fields[1].append(field)
            fields[2].append(value * field)
        for slot in range(3):
            for j, tile in enumerate(smooth_lanes(fields[slot])):
                smooth[slot, j, plane, rows, :] = tile
        return fields[0]

    def sweep_own(plane, _):
        for k in range(CY // 16):
            rows = pl.ds(pl.multiple_of(own + 16 * k, 8), 16)
            for j, tile in enumerate(sweep_lines(plane, rows, 16)):
                stiff[j, plane, rows, :] = tile
        return 0

    def volume_plane(plane, total):
        for j in range(TILES):
            here = lab_out[plane, :, 128 * j : 128 * j + 128] == 0
            value = jnp.where(here, ud[1, j, plane + 1, mine_rows, :], 0.0)
            total = total + jnp.sum(value.reshape(CY // 8, 8, 128), axis=0)
        return total

    pl.semaphore_wait(barrier, len(greeted))
    start(0)
    for copy in side_copies:
        copy.start()
    tell(0)
    lax.fori_loop(0, TILES, clear, 0)
    for copy in loads[3:]:
        copy.wait()
    volume = lax.fori_loop(0, CZ, volume_plane, jnp.zeros((8, 128), F32))
    lax.fori_loop(1, 4, sweep_own, 0)
    sent(0)
    start(1)
    lax.fori_loop(4, 6, sweep_own, 0)
    heard(0)
    tell(1)

    def across(ref, j, plane, start, rows):
        over = ref[j, plane - 1, pl.ds(start, rows), :] + ref[j, plane + 1, pl.ds(start, rows), :]
        return over + (ref[j, plane, pl.ds(start - 1, rows), :] + ref[j, plane, pl.ds(start + 1, rows), :])

    def factor(row, j, rows):
        return jnp.broadcast_to(factors[row : row + 1, 128 * j : 128 * j + 128], (rows, 128))

    body = pl.ds(8, 72)

    def put(ref, j, plane, value, keep):
        ref[j, plane, body, :] = value if keep is None else value * keep

    def level3(plane, keep=None):
        for j in range(TILES):
            value = factor(0, j, 72) * e[j, plane, body, :] - (2.0 * NEAR * GAMMA[4]) * across(e, j, plane, 8, 72)
            put(b3, j, plane, value, keep)

    def level2(plane, keep=None):
        for j in range(TILES):
            value = (GAMMA[2] - GAMMA[4]) * e[j, plane, body, :] + factor(1, j, 72) * b3[j, plane, body, :]
            put(b2, j, plane, value - (2.0 * NEAR) * across(b3, j, plane, 8, 72), keep)

    def level1(plane, keep=None):
        for j in range(TILES):
            value = GAMMA[1] * e[j, plane, body, :] + factor(1, j, 72) * b2[j, plane, body, :]
            value = value - b3[j, plane, body, :]
            put(b1, j, plane, value - (2.0 * NEAR) * across(b2, j, plane, 8, 72), keep)

    def level0(plane, slot):
        for j in range(TILES):
            value = GAMMA[0] * e[j, plane, mine_rows, :] + factor(2, j, CY) * b1[j, plane, mine_rows, :]
            value = value - b2[j, plane, mine_rows, :]
            flat[slot, :, 128 * j : 128 * j + 128] = value - NEAR * across(b1, j, plane, own, CY)

    def repeat(level, first, last):
        def step(plane, _):
            level(plane)
            return 0

        lax.fori_loop(first, last, step, 0)

    side_copies[0].wait_recv()
    repeat(level3, 5, 11)
    repeat(level2, 6, 10)
    repeat(level1, 7, 9)
    side_copies[1].wait_recv()
    side_copies[2].wait_recv()
    heard(1)
    tell(2)

    sent(1)
    for copy in ud_copies:
        copy.start()
    low_keep = jnp.where(z == 0, 0.0, 1.0).astype(F32)
    high_keep = jnp.where(z == GZ - 1, 0.0, 1.0).astype(F32)

    def keep_of(plane):
        return low_keep if plane < DEEP else high_keep if plane >= DEEP + CZ else None

    def back(first, count, planes, total):
        value = transform(flat[first : first + count].reshape(count * CY, NX), basis)
        for k, plane in enumerate(planes):
            kept = jnp.where(lab_out[plane] == 0, value[CY * k : CY * k + CY], 0.0)
            filt_out[plane] = kept
            total = total + jnp.sum(jnp.abs(kept).reshape(CY // 8, 8, NX), axis=0)
        return total

    total = jnp.zeros((8, NX), F32)
    order = []
    for d in range(1, DEEP + 1):
        if d in FIRSTS:
            up_copies[FIRSTS[d]].wait_recv()
            down_copies[FIRSTS[d]].wait_recv()

        @pl.when(z == 0)
        def _():
            e[:, DEEP - d] = jnp.zeros((TILES, ROWS, 128), F32)

        @pl.when(z == GZ - 1)
        def _():
            e[:, DEEP + CZ - 1 + d] = jnp.zeros((TILES, ROWS, 128), F32)

        for level, low in ((level3, 5 - d), (level2, 6 - d), (level1, 7 - d)):
            for plane in (low, FZ - 1 - low):
                level(plane, keep_of(plane))
        for low in (8 - d, FZ - 1 - (8 - d)):
            level0(low, len(order))
            order.append(low - DEEP)
        if d == DEEP - 1:
            total = back(0, 6, order, total)
    total = back(6, 2, order[6:], total)

    def fold(value):
        return jnp.sum(value, axis=0, keepdims=True)

    row = lax.broadcasted_iota(jnp.int32, (8, 128), 0)
    size = total[:, :128] + total[:, 128:256] + total[:, 256:384] + total[:, 384:]
    mine[0] = jnp.where(row < 4, fold(size), fold(volume))

    def spread(phase):
        for d in range(GROUP - 1):
            remote(mine.at[phase], got.at[phase, d], ar_send.at[phase], ar_recv.at[phase], groups[phase][d]).start()

    def gather(phase):
        pltpu.make_async_copy(got.at[phase], got.at[phase], ar_recv.at[phase]).wait()
        return mine[phase] + jnp.sum(got[phase], axis=0)

    heard(2)
    spread(0)

    lax.fori_loop(6, CZ + 1, sweep_own, 0)
    def sweep_out(plane, _):
        for slot in range(3):
            for j in range(TILES):
                column[slot, j, body, :] = smooth[slot, j, plane + 1, body, :] + 0.5 * (
                    smooth[slot, j, plane, body, :] + smooth[slot, j, plane + 2, body, :]
                )
        for j in range(TILES):
            lanes = slice(128 * j, 128 * j + 128)

            def stack(slot):
                return column[slot, j, mine_rows, :] + 0.5 * (
                    column[slot, j, pl.ds(own - 1, CY), :] + column[slot, j, pl.ds(own + 1, CY), :]
                )

            value = stiff[j, plane + 1, mine_rows, :]
            field = ud[0, j, plane + 1, mine_rows, :]
            diagonal = 6.0 * value + stack(0)
            offsum = value * (stack(1) - 2.0 * field) + stack(2)
            applied = diagonal * field - offsum
            updated = field + relax_omega * (load_v[plane, :, lanes] - applied) / diagonal
            adj_out[plane, :, lanes] = jnp.where(lab_out[plane, :, lanes] == 2, 0.0, updated)
        return 0

    mine[1] = gather(0)
    spread(1)

    for copy in ud_copies:
        copy.wait_recv()

    for plane, keep in ((0, low_keep), (CZ + 1, high_keep)):
        for k in range(3):
            sweep_lines(plane, pl.ds(8 + 24 * k, 24), 24, keep)

    def sweep_partner(plane, _):
        sweep_lines(plane, partner, 8)
        return 0

    lax.fori_loop(1, CZ + 1, sweep_partner, 0)

    lax.fori_loop(0, CZ, sweep_out, 0)

    tot_out[...] = gather(1)
    for phase in range(2):
        pltpu.make_async_copy(got.at[phase], got.at[phase], ar_send.at[phase]).wait()
    for copy in side_copies + ud_copies:
        copy.wait_send()


def last_kernel(filt, adj_in, labels, tot, dir_out, adj_out, held, sem):
    whole = pltpu.make_async_copy(adj_in, adj_out, sem.at[CZ])
    whole.start()
    cells = float(GZ * CZ * GY * CY * NX)
    magnitude = jnp.sum(tot[0:1, :], axis=1, keepdims=True)
    volume = jnp.sum(tot[4:5, :], axis=1, keepdims=True)
    scale = 1.0 / (magnitude / cells + epsilon)
    offset = volume_penalty * (volume / cells - volume_target)
    scale = jnp.broadcast_to(scale, (CY, NX))
    offset = jnp.broadcast_to(offset, (CY, NX))
    copies = []
    for plane in range(CZ):
        held[plane] = jnp.where(labels[plane] == 0, filt[plane] * scale - offset, 0.0)
        copy = pltpu.make_async_copy(held.at[plane], dir_out.at[plane], sem.at[plane])
        copy.start()
        copies.append(copy)
    for copy in copies + [whole]:
        copy.wait()


def on_device(sensitivity, density, load, adjoint, labels):
    shape = (CZ, CY, NX)
    dma = pltpu.SemaphoreType.DMA
    vmem = pl.BlockSpec(memory_space=pltpu.VMEM)
    hbm = pl.BlockSpec(memory_space=pltpu.HBM)
    arrays = (sensitivity, density, load, adjoint, labels, jnp.asarray(BASIS), jnp.asarray(FACTORS))
    filtered, swept, held_labels, totals = pl.pallas_call(
        main_kernel,
        out_shape=(
            pltpu.VMEM(shape, F32),
            pltpu.VMEM(shape, F32),
            pltpu.VMEM(shape, jnp.int32),
            pltpu.VMEM((8, 128), F32),
        ),
        in_specs=[hbm] * 7,
        out_specs=(vmem,) * 4,
        scratch_shapes=[
            pltpu.VMEM(shape, F32),
            pltpu.VMEM((2, NX, NX), jnp.bfloat16),
            pltpu.VMEM((8, NX), F32),
            pltpu.VMEM((TILES, FZ, ROWS, 128), F32),
            pltpu.VMEM((TILES, FZ, ROWS, 128), F32),
            pltpu.VMEM((TILES, FZ, ROWS, 128), F32),
            pltpu.VMEM((TILES, FZ, ROWS, 128), F32),
            pltpu.VMEM(shape, F32),
            pltpu.VMEM((2, TILES, CZ + 2, ROWS, 128), F32),
            pltpu.VMEM((TILES, CZ + 2, ROWS, 128), F32),
            pltpu.VMEM((3, TILES, CZ + 2, ROWS, 128), F32),
            pltpu.VMEM((3, TILES, ROWS, 128), F32),
            pltpu.VMEM(shape, F32),
            pltpu.VMEM((2, 8, 128), F32),
            pltpu.VMEM((2, GROUP - 1, 8, 128), F32),
            dma((5 + 2 * TILES,)),
            dma((len(PIECES),)),
            dma((len(PIECES),)),
            dma((len(PIECES),)),
            dma((len(PIECES),)),
            dma((3,)),
            dma((3,)),
            dma((5,)),
            dma((5,)),
            dma((2,)),
            dma((2,)),
            pltpu.SemaphoreType.REGULAR((3,)),
        ],
        compiler_params=pltpu.CompilerParams(
            collective_id=1, has_side_effects=True, vmem_limit_bytes=40 * 2**20
        ),
        name="filter_and_sweep",
    )(*[pltpu.with_memory_space_constraint(array, pltpu.HBM) for array in arrays])
    filtered, swept, held_labels, totals = (
        pltpu.with_memory_space_constraint(array, pltpu.VMEM) for array in (filtered, swept, held_labels, totals)
    )
    return pl.pallas_call(
        last_kernel,
        out_shape=(jax.ShapeDtypeStruct(shape, F32), jax.ShapeDtypeStruct(shape, F32)),
        in_specs=[vmem] * 4,
        out_specs=(hbm, hbm),
        scratch_shapes=[pltpu.VMEM(shape, F32), dma((CZ + 1,))],
        name="normalise_and_store",
    )(filtered, swept, held_labels, totals)


def solution(mesh):
    placed = (P("gz", "gy", None),) * 5
    return jax.shard_map(
        on_device,
        mesh=mesh,
        in_specs=placed,
        out_specs=(P("gz", "gy", None), P("gz", "gy", None)),
        check_vma=False,
    )
```
